128 devices in a mesh: col: 16 (over y_hi, x, core), band: 8 (over z, y_lo).
Axes of the slice: x: 4, y: 4 (y_hi: 2, y_lo: 2; y = y_hi * 2 + y_lo), z: 4, core: 2. Of those that a mesh axis runs over, the one named last changes fastest.
Arguments:
- left_view: bfloat16 [320, 8, 4096], P(None, 'band', 'col'), may hold values from -6 to 6
- right_view: bfloat16 [320, 8, 4096], P(None, 'band', 'col'), may hold values from -6 to 6
- first_weight: bfloat16 [3, 3, 320, 320], replicated, may hold values from -0.109375 to 0.109375
- second_weight: bfloat16 [3, 3, 320, 320], replicated, may hold values from -0.109375 to 0.109375
- agg_weight: bfloat16 [3, 3, 32, 3, 40], replicated, may hold values from -0.1875 to 0.1875
Outputs:
- aggregated: bfloat16 [32, 192, 8, 4096], P(None, 'band', None, 'col')
The draws below stay inside these ranges and needn't reach their ends.
All inputs are finite; a program needn't handle non-finite values.
Results may differ from the reference program's by a relative error of at most 0.0067.
Values may be sent and summed in bfloat16 or wider, within the bound.
No kernel may reach another device: no remote copies, remote signals or barrier semaphores. Data moves between devices by JAX's collectives and lax.ppermute only.
A program may use at most 256 MiB of HBM per device.

```python
import jax
import jax.numpy as jnp
from jax import lax

C = 320
G = 40
D = 192
F = 32
H = 8
W = 4096
N_BAND = 8


def level_of(key, extent, cuts, low, top_value):
    level, own = 1.0, jax.random.fold_in(key, 6)
    for axis_at, parts in cuts:
        draws = jnp.exp(jax.random.uniform(jax.random.fold_in(own, axis_at), (parts,), jnp.float32, low / len(cuts), top_value / len(cuts)))
        level = level * jnp.repeat(draws, extent[axis_at] // parts).reshape([-1 if axis == axis_at else 1 for axis in range(len(extent))])
    return level


def bell_draw(rng, extent, deviation, limit, pieces=(), held_as=jnp.bfloat16):
    drawn = jax.random.normal(rng, extent, jnp.float32) * deviation
    if len(pieces) > 0:
        drawn = level_of(rng, extent, pieces, -0.22, 0.18) * drawn
    return jnp.clip(drawn, min=-limit, max=limit).astype(held_as)


def setup_inputs(seed: int = 0) -> dict:
    key_of = jax.random.split(jax.random.key(seed), 6)
    left_view = bell_draw(key_of[0], (C, H, W), 1.0, 6.0, ((1, 8), (2, 16)))
    right_view = bell_draw(key_of[1], (C, H, W), 1.0, 6.0, ((1, 8), (2, 16)))
    first_weight = bell_draw(key_of[2], (3, 3, C, C), (9 * C) ** -0.5, 0.109375)
    second_weight = bell_draw(key_of[3], (3, 3, C, C), (9 * C) ** -0.5, 0.109375)
    agg_weight = bell_draw(key_of[4], (3, 3, F, 3, G), (27 * G) ** -0.5, 0.1875)
    return dict(left_view=left_view, right_view=right_view, first_weight=first_weight, second_weight=second_weight, agg_weight=agg_weight)


def conv_plane(views, weight):
    height = views.shape[2]
    width = views.shape[3]
    padded = jnp.pad(views, ((0, 0), (0, 0), (1, 1), (1, 1))).astype(jnp.float32)
    summed = jnp.zeros((views.shape[0], weight.shape[2], height, width), jnp.float32)
    for row_tap in range(3):
        for col_tap in range(3):
            summed = summed + jnp.einsum("oc,vchw->vohw", weight[row_tap, col_tap].astype(jnp.float32),
                                         padded[:, :, row_tap:row_tap + height, col_tap:col_tap + width])
    return summed


def aggregate(padded, weight):
    depth = padded.shape[0] - 2
    height = padded.shape[2] - 2
    width = padded.shape[3] - 2
    summed = jnp.zeros((weight.shape[2], depth, height, width), jnp.float32)
    for row_tap in range(3):
        stacked = jnp.stack([padded[:, :, row_tap:row_tap + height, col_tap:col_tap + width]
                             for col_tap in range(3)], axis=1).astype(jnp.float32)
        for disp_tap in range(3):
            summed = summed + jnp.einsum("fkg,dkghw->fdhw", weight[disp_tap, row_tap].astype(jnp.float32),
                                         stacked[disp_tap:disp_tap + depth])
    return summed


def reference(left_view, right_view, first_weight, second_weight, agg_weight):
    views = jnp.stack([left_view, right_view])
    hidden = jax.nn.relu(conv_plane(views, first_weight)).astype(jnp.bfloat16)
    features = (views.astype(jnp.float32) + conv_plane(hidden, second_weight)).astype(jnp.bfloat16)
    left_feat = features[0].astype(jnp.float32)
    right_pad = jnp.pad(features[1], ((0, 0), (0, 0), (D, 0))).astype(jnp.float32)
    band_size = D // N_BAND

    def one_band(band_number):
        band_first = band_number * band_size

        def one_disp(offset):
            disparity = band_first - 1 + offset
            inside = ((disparity >= 0) & (disparity < D)).astype(jnp.float32)
            clipped = jnp.clip(disparity, 0, D - 1).astype(jnp.int32)
            shifted = lax.dynamic_slice_in_dim(right_pad, (D - clipped).astype(jnp.int32), W, 2)
            products = left_feat * shifted
            return products.reshape(G, C // G, H, W).mean(axis=1) * inside

        volume = lax.map(one_disp, jnp.arange(band_size + 2, dtype=jnp.int32)).astype(jnp.bfloat16)
        padded = jnp.pad(volume, ((0, 0), (0, 0), (1, 1), (1, 1)))
        return jax.nn.relu(aggregate(padded, agg_weight)).astype(jnp.bfloat16)

    bands = lax.map(one_band, jnp.arange(N_BAND, dtype=jnp.int32))
    return jnp.transpose(bands, (1, 0, 2, 3, 4)).reshape(F, D, H, W)
```

```python
import functools

import jax
import jax.numpy as jnp
from jax import lax
from jax.experimental import pallas as pl
from jax.experimental.pallas import tpu as pltpu
from jax.sharding import PartitionSpec as P

G, J, D, F, H, WL, BD, C, W = 40, 8, 192, 32, 8, 256, 24, 320, 4096
CH = J * H * G
REM = 144
ML, MR = 272, 288
LR, RR = 272, 296
NT = BD + 2
KT = 3 * 384

def build(dst, slot, src, m):
    for n in range(2):
        for e in range(3):
            dst[slot, :, (n * 3 + e) * 128:(n * 3 + e + 1) * 128] = src(n, e).astype(jnp.bfloat16)
    lane = lax.broadcasted_iota(jnp.int32, (m, 128), 1)
    pair = jnp.where(lane < 64, src(2, 0), pltpu.roll(src(2, 1), 64, 1))
    dst[slot, :, 768:896] = pair.astype(jnp.bfloat16)
    dst[slot, :, 896:960] = src(2, 2)[:, :64].astype(jnp.bfloat16)

def conv_kernel(m, s_ref, *refs):
    xin = refs[:8]
    wm1, wr1, wm2, wr2, out_ref, raw, xs, hs, ts, z, feat = refs[8:]
    k, base = s_ref[0], s_ref[1]
    for d in range(8):
        h = jnp.bitwise_xor(k, d)
        for n in range(2):
            raw[h, n, 0:m, :] = xin[d][n * m:n * m + m, :].astype(jnp.float32)
        rem = xin[d][2 * m:2 * m + REM, :].astype(jnp.float32)
        raw[h, 2, 0:REM, :] = rem
        raw[h, 2, m - REM:m, :] = pltpu.roll(rem, 64, 1)
    for slot in (0, 9):
        xs[slot] = jnp.zeros((m, 960), jnp.bfloat16)
        hs[slot] = jnp.zeros((m, 960), jnp.bfloat16)
        z[slot] = jnp.zeros((2, m, 128), jnp.float32)
    col = base + lax.broadcasted_iota(jnp.int32, (m, 128), 0)

    def rest(x, wr, h):
        y = jnp.dot(x[h + 1], wr[...], preferred_element_type=jnp.float32)
        z[h + 1, 0] = y[:, :128]
        z[h + 1, 1, :, 0:64] = y[:, 128:192]

    def conv(x, wm, h):
        y = jnp.dot(x[h], wm[0], preferred_element_type=jnp.float32)
        y += jnp.dot(x[h + 1], wm[1], preferred_element_type=jnp.float32)
        y += jnp.dot(x[h + 2], wm[2], preferred_element_type=jnp.float32)
        return y[:, :128], y[:, 128:], z[h, 0] + pltpu.roll(z[h + 1, 0], 64, 1) + z[h + 2, 1]

    def load(h, c):
        build(xs, h + 1, lambda n, e: raw[h, n, e:e + m, :], m)
        rest(xs, wr1, h)
        return c
    lax.fori_loop(0, H, load, 0)
    def first(h, c):
        ok = jnp.logical_and(col + 1 >= 0, col + 1 < W)
        for n, y in enumerate(conv(xs, wm1, h)):
            ts[n, 0:m, :] = jnp.where(ok, jnp.maximum(y, 0.0), 0.0)
        build(hs, h + 1, lambda n, e: ts[n, e:e + m, :], m)
        return c
    lax.fori_loop(0, H, first, 0)
    def rest2(h, c):
        rest(hs, wr2, h)
        return c
    lax.fori_loop(0, H, rest2, 0)
    def second(h, c):
        ok = jnp.logical_and(col + 2 >= 0, col + 2 < W)
        for n, y in enumerate(conv(hs, wm2, h)):
            y = jnp.where(ok, y + raw[h, n, 2:2 + m, :], 0.0)
            feat[h, n] = y.astype(jnp.bfloat16).astype(jnp.float32)
        return c
    lax.fori_loop(0, H, second, 0)

    lane = lax.broadcasted_iota(jnp.int32, (16, 128), 1)
    def place(i, c):
        row = pl.multiple_of(i * 16, 16)
        for q in range(20):
            got = None
            for j in range(J):
                for h in range(H):
                    t0 = j * H * G + h * G
                    lo, hi = max(t0, q * 128), min(t0 + G, q * 128 + 128)
                    if lo >= hi:
                        continue
                    s_lo = lo - t0 + j * G
                    while lo < hi:
                        n = s_lo // 128
                        length = min(hi - lo, (n + 1) * 128 - s_lo)
                        x = feat[h, n, pl.ds(row, 16), :]
                        sh = (lo - s_lo) % 128
                        if sh:
                            x = pltpu.roll(x, sh, 1)
                        got = x if got is None else jnp.where(lane >= lo - q * 128, x, got)
                        lo, s_lo = lo + length, s_lo + length
            out_ref[pl.ds(row, 16), q * 128:q * 128 + 128] = got.astype(jnp.bfloat16)
        return c
    lax.fori_loop(0, m // 16, place, 0)

def conv_call(m, scal, xs, weights):
    return pl.pallas_call(
        functools.partial(conv_kernel, m),
        out_shape=jax.ShapeDtypeStruct((m, CH), jnp.bfloat16),
        in_specs=[pl.BlockSpec(memory_space=pltpu.SMEM)] + [pl.BlockSpec(memory_space=pltpu.VMEM)] * 12,
        out_specs=pl.BlockSpec(memory_space=pltpu.VMEM),
        scratch_shapes=[pltpu.VMEM((8, 3, m + 8, 128), jnp.float32), pltpu.VMEM((10, m, 960), jnp.bfloat16),
                        pltpu.VMEM((10, m, 960), jnp.bfloat16), pltpu.VMEM((3, m + 8, 128), jnp.float32),
                        pltpu.VMEM((10, 2, m, 128), jnp.float32), pltpu.VMEM((8, 3, m, 128), jnp.float32)],
        compiler_params=pltpu.CompilerParams(vmem_limit_bytes=56 * 2**20),
        name="feature_block",
    )(scal, *xs, *weights)

def group_major(x, axis):
    shape = x.shape
    x = x.reshape(shape[:axis] + (G, J) + shape[axis + 1:])
    return jnp.swapaxes(x, axis, axis + 1).reshape(shape)

def conv_weights(w):
    a = w.transpose(0, 1, 3, 2)
    main = a[:, :, :256].reshape(3, 3, 2, 128, C).transpose(0, 2, 1, 3, 4).reshape(3, 768, C)
    full = jnp.concatenate([main, a[:, :, 256:].reshape(3, 192, C)], axis=1)
    return full[:, :, :256], full[:, :, 256:].transpose(1, 0, 2).reshape(960, 192)

def pack(a):
    m = a.shape[0]
    return jnp.concatenate([a[:, :128], a[:, 128:256],
        jnp.concatenate([a[:REM, 256:], a[m - REM:, 256:]], axis=1)], axis=0)

def corr2(l_ref, r_ref, v_ref, p):
    def tile(i, c):
        row = pl.multiple_of(i * 8, 8)
        q = [[None] * 5 for _ in range(2)]
        for m in range(4):
            for n in range(5):
                lt = l_ref[m * 5 + n, pl.ds(row, 8), :]
                for u in range(2):
                    pr = lt * r_ref[m * 5 + n, pl.ds(row + (25 - u) - 2 * p, 8), :]
                    q[u][n] = pr if m == 0 else q[u][n] + pr
        for u in range(2):
            x = jnp.concatenate(q[u], axis=1)
            x = x + pltpu.roll(x, 320, 1)
            for n in range(3):
                v_ref[u, n, pl.ds(row, 8), :] = x[:, n * 128:n * 128 + 128]
        return c
    lax.fori_loop(0, 33, tile, 0, unroll=3)

def agg_kernel(k_ref, l_ref, r_ref, b_ref, out_ref, lf_ref, rf_ref, v_ref, vs_ref):
    k = k_ref[0]
    for n in range(20):
        lf_ref[n] = l_ref[:, n * 128:n * 128 + 128].astype(jnp.float32)
        rf_ref[n, 0:MR, :] = r_ref[:, n * 128:n * 128 + 128].astype(jnp.float32)
    def pair(p, c):
        corr2(lf_ref, rf_ref, v_ref, p)
        for u in range(2):
            t = 2 * p + u
            d = 24 * k - 1 + t
            ok = jnp.logical_and(d >= 0, d < D)
            m = jnp.where(ok, 1.0, 0.0).astype(jnp.float32)
            for e in range(3):
                for n in range(3):
                    vs_ref[t, :, e * 384 + n * 128:e * 384 + n * 128 + 128] = (v_ref[u, n, e:e + WL, :] * m).astype(jnp.bfloat16)
        return c
    lax.fori_loop(0, NT // 2, pair, 0)
    def out(d, c):
        y = jnp.dot(vs_ref[d], b_ref[0], preferred_element_type=jnp.float32)
        y += jnp.dot(vs_ref[d + 1], b_ref[1], preferred_element_type=jnp.float32)
        y += jnp.dot(vs_ref[d + 2], b_ref[2], preferred_element_type=jnp.float32)
        y = jnp.maximum(y, 0.0).T.reshape(F, H, WL)
        out_ref[:, d] = y.astype(jnp.bfloat16)
        return c
    lax.fori_loop(0, BD, out, 0)

def agg_rhs(w):
    w = w * jnp.asarray(0.125, w.dtype)
    z = jnp.zeros((3, F, 3, G), w.dtype)
    cols = []
    for hi in range(H):
        rows = [w[:, hi + 1 - ho] if 0 <= hi + 1 - ho <= 2 else z for ho in range(H)]
        cols.append(jnp.stack(rows, axis=2))
    full = jnp.stack(cols, axis=4)
    full = full.transpose(0, 3, 4, 5, 1, 2).reshape(3, 3, H * G, F * H)
    full = jnp.pad(full, ((0, 0), (0, 0), (0, 64), (0, 0)))
    return full.reshape(3, KT, F * H)

def agg_call(k, lx, rx, b):
    return pl.pallas_call(
        agg_kernel,
        out_shape=jax.ShapeDtypeStruct((F, BD, H, WL), jnp.bfloat16),
        in_specs=[pl.BlockSpec(memory_space=pltpu.SMEM)] + [pl.BlockSpec(memory_space=pltpu.VMEM)] * 3,
        out_specs=pl.BlockSpec(memory_space=pltpu.VMEM),
        scratch_shapes=[pltpu.VMEM((20, LR, 128), jnp.float32), pltpu.VMEM((20, RR, 128), jnp.float32),
                        pltpu.VMEM((2, 3, LR, 128), jnp.float32), pltpu.VMEM((NT, WL, KT), jnp.bfloat16)],
        compiler_params=pltpu.CompilerParams(vmem_limit_bytes=56 * 2**20),
        name="correlate_aggregate",
    )(k, lx, rx, b)


def from_col(x, by):
    n = lax.axis_size("col")
    return lax.ppermute(x, "col", [(i, i + by) for i in range(n) if 0 <= i + by < n])


def to_band(x, d):
    return lax.ppermute(x, "band", [(i, i ^ d) for i in range(lax.axis_size("band"))])


def shards(left_view, right_view, first_weight, second_weight, agg_weight):
    k = lax.axis_index("band")
    c = lax.axis_index("col")
    left = group_major(left_view[:, 0], 0).T
    right = group_major(right_view[:, 0], 0).T
    before = from_col(jnp.concatenate([left[WL - 16:], right[WL - 208:]], axis=0), 1)
    after = from_col(jnp.concatenate([left[:16], right[:16]], axis=0), -1)
    left = jnp.concatenate([before[13:16], left, after[:13]], axis=0)
    right = jnp.concatenate([before[16:], right, after[16:]], axis=0)
    packed = pack(left)
    lefts = [packed] + [to_band(packed, d) for d in range(1, 8)]

    def window(d):
        start = 181 - BD * jnp.bitwise_xor(k, d)
        return pack(lax.dynamic_slice_in_dim(right, start, MR, 0))

    rights = [window(0)] + [to_band(window(d), d) for d in range(1, 8)]
    weights = (*conv_weights(group_major(first_weight, 3)), *conv_weights(group_major(second_weight, 2)))
    base = c * WL
    lf = conv_call(ML, jnp.stack([k, base - 3]).astype(jnp.int32), lefts, weights)
    rf = conv_call(MR, jnp.stack([k, base - BD * k - 27]).astype(jnp.int32), rights, weights)
    return agg_call(k[None].astype(jnp.int32), lf, rf, agg_rhs(agg_weight))


def solution(mesh):
    return jax.shard_map(
        shards,
        mesh=mesh,
        in_specs=(P(None, "band", "col"), P(None, "band", "col"), P(), P(), P()),
        out_specs=P(None, "band", None, "col"),
        check_vma=False,
    )
```

```python
import functools

import jax
import jax.numpy as jnp
import numpy as np
from jax import lax
from jax.experimental import pallas as pl
from jax.experimental.pallas import tpu as pltpu
from jax.sharding import PartitionSpec as P

G, J, D, F, H, WL, BD, C, W = 40, 8, 192, 32, 8, 256, 24, 320, 4096
CH = J * H * G
REM = 144
ML, MR = 272, 288
LR, RR = 272, 296
NT = BD + 2
KT = 3 * 384

def dot_nt(x, w):
    return lax.dot_general(x, w, (((1,), (1,)), ((), ())), preferred_element_type=jnp.float32)

def build(dst, slot, src, m):
    for n in range(2):
        for e in range(3):
            dst[slot, :, (n * 3 + e) * 128:(n * 3 + e + 1) * 128] = src(n, e).astype(jnp.bfloat16)
    lane = lax.broadcasted_iota(jnp.int32, (m, 128), 1)
    pair = jnp.where(lane < 64, src(2, 0), pltpu.roll(src(2, 1), 64, 1))
    dst[slot, :, 768:896] = pair.astype(jnp.bfloat16)
    dst[slot, :, 896:960] = src(2, 2)[:, :64].astype(jnp.bfloat16)

def conv_kernel(m, at, s_ref, *refs):
    xin = refs[:8]
    wm1, wr1, wm2, wr2, order, out_ref, raw, xs, hs, ts, z, fb, feat, wide = refs[8:]
    k, base = s_ref[0], s_ref[1]
    y = k & 1
    if at:
        start = window_start(k)
        formats = [(FULL, start)] * 2 + [(288, 0)] * 2 + [(PAIR, 24 - 24 * y), (288, 0), (288, 0), (PAIR, 24 - 24 * y)]
    else:
        formats = [(m, 0)] * 8
    source = [k, k ^ 1, (k + 6) & 7, (k + 2) & 7, (k + 4) & 7, ((k + 6) & 7) ^ 1, ((k + 2) & 7) ^ 1, ((k + 4) & 7) ^ 1]
    for d in range(8):
        h, (size, start) = source[d], formats[d]
        rem = REM if size == m else size // 2
        if size == m:
            uncut(raw.at[h], xin[d], at, m, rem)
        else:
            uncut(wide, xin[d], at, size, rem)
            for n in range(3):
                raw[h, n, 0:m, :] = wide[n, pl.ds(start, m), :]
    for slot in (0, 9):
        xs[slot] = jnp.zeros((m, 960), jnp.bfloat16)
        hs[slot] = jnp.zeros((m, 960), jnp.bfloat16)
        z[slot] = jnp.zeros((2, m, 128), jnp.float32)
    col = base + lax.broadcasted_iota(jnp.int32, (m, 128), 0)

    def rest(x, wr, h):
        y = dot_nt(x[h + 1], wr[...])
        z[h + 1, 0] = y[:, :128]
        z[h + 1, 1, :, 0:64] = y[:, 128:192]

    def conv(x, wm, h):
        y = dot_nt(x[h], wm[0])
        y += dot_nt(x[h + 1], wm[1])
        y += dot_nt(x[h + 2], wm[2])
        return y[:, :128], y[:, 128:], z[h, 0] + pltpu.roll(z[h + 1, 0], 64, 1) + z[h + 2, 1]

    def load(h, c):
        build(xs, h + 1, lambda n, e: raw[h, n, e:e + m, :], m)
        rest(xs, wr1, h)
        return c
    lax.fori_loop(0, H, load, 0)
    def first(h, c):
        ok = jnp.logical_and(col + 1 >= 0, col + 1 < W)
        for n, y in enumerate(conv(xs, wm1, h)):
            ts[n, 0:m, :] = jnp.where(ok, jnp.maximum(y, 0.0), 0.0)
        build(hs, h + 1, lambda n, e: ts[n, e:e + m, :], m)
        return c
    lax.fori_loop(0, H, first, 0)
    def rest2(h, c):
        rest(hs, wr2, h)
        return c
    lax.fori_loop(0, H, rest2, 0)
    def second(h, c):
        ok = jnp.logical_and(col + 2 >= 0, col + 2 < W)
        for n, y in enumerate(conv(hs, wm2, h)):
            y = jnp.where(ok, y + raw[h, n, 2:2 + m, :], 0.0)
            if n < 2:
                fb[:, n * 128:n * 128 + 128] = y.astype(jnp.bfloat16)
            else:
                fb[:, 256:320] = y[:, :64].astype(jnp.bfloat16)
        y = jnp.dot(fb[...], order[...], preferred_element_type=jnp.float32)
        for n in range(3):
            feat[h, n] = y[:, n * 128:n * 128 + 128]
        return c
    lax.fori_loop(0, H, second, 0)

    lane = lax.broadcasted_iota(jnp.int32, (16, 128), 1)
    def place(i, c):
        row = pl.multiple_of(i * 16, 16)
        for q in range(20):
            got = None
            for j in range(J):
                for h in range(H):
                    t0 = j * H * G + h * G
                    lo, hi = max(t0, q * 128), min(t0 + G, q * 128 + 128)
                    if lo >= hi:
                        continue
                    x = feat[h, j // 3, pl.ds(row, 16), :]
                    sh = (t0 - (j % 3) * G) % 128
                    if sh:
                        x = pltpu.roll(x, sh, 1)
                    got = x if got is None else jnp.where(lane >= lo - q * 128, x, got)
            out_ref[pl.ds(row, 16), q * 128:q * 128 + 128] = got.astype(jnp.bfloat16)
        return c
    lax.fori_loop(0, m // 16, place, 0)

def conv_call(m, at, scal, xs, weights):
    return pl.pallas_call(
        functools.partial(conv_kernel, m, at),
        out_shape=jax.ShapeDtypeStruct((m, CH), jnp.bfloat16),
        in_specs=[pl.BlockSpec(memory_space=pltpu.SMEM)] + [pl.BlockSpec(memory_space=pltpu.VMEM)] * 13,
        out_specs=pl.BlockSpec(memory_space=pltpu.VMEM),
        scratch_shapes=[pltpu.VMEM((8, 3, m + 8, 128), jnp.float32), pltpu.VMEM((10, m, 960), jnp.bfloat16),
                        pltpu.VMEM((10, m, 960), jnp.bfloat16), pltpu.VMEM((3, m + 8, 128), jnp.float32),
                        pltpu.VMEM((10, 2, m, 128), jnp.float32), pltpu.VMEM((m, C), jnp.bfloat16), pltpu.VMEM((8, 3, m, 128), jnp.float32), pltpu.VMEM((3, 480, 128), jnp.float32)],
        compiler_params=pltpu.CompilerParams(vmem_limit_bytes=56 * 2**20),
        cost_estimate=pl.CostEstimate(flops=2 * 18 * m * H * C * C * 2, bytes_accessed=6_000_000, transcendentals=0),
        name="feature_block",
    )(scal, *xs, *weights)

def order_matrix():
    lane = np.arange(384)
    j, g = 3 * (lane // 128) + (lane % 128) // G, (lane % 128) % G
    hit = (np.arange(C)[:, None] == (g * J + j)[None, :]) & (lane % 128 < 3 * G)[None, :] & (j < J)[None, :]
    return jnp.asarray(hit, jnp.bfloat16)

def weights_kernel(w1, w2, aw, wm1, wr1, wm2, wr2, bt, tmp):
    lane = lax.broadcasted_iota(jnp.int32, (C, 128), 1)
    for w, wm, wr in ((w1, wm1, wr1), (w2, wm2, wr2)):
        for b in range(3):
            def put(at, width, x, b=b, wm=wm, wr=wr):
                wm[b, :, at:at + width] = x[:256]
                wr[b * 64:b * 64 + 64, at:at + width] = x[256:]
            for e in range(3):
                for n in range(2):
                    put((n * 3 + e) * 128, 128, w[b * 3 + e, :, n * 128:n * 128 + 128])
            zero = jnp.zeros((C, 64), jnp.float32)
            last = [jnp.concatenate([w[b * 3 + e, :, 256:320].astype(jnp.float32), zero], axis=1) for e in range(3)]
            pair = jnp.where(lane < 64, last[0], pltpu.roll(last[1], 64, 1))
            put(768, 128, pair.astype(jnp.bfloat16))
            put(896, 64, w[b * 3 + 2, :, 256:320])
    wide = lax.broadcasted_iota(jnp.int32, (F, 384), 1)
    for a in range(3):
        for e in range(3):
            x = jnp.concatenate([aw[a * 3 + e].astype(jnp.float32), jnp.zeros((F, 264), jnp.float32)], axis=1) * 0.125
            for ho in range(H):
                y = x if ho == 1 else pltpu.roll(x, ((ho - 1) * G) % 384, 1)
                y = jnp.where(wide < H * G, y, 0.0)
                for n in range(3):
                    tmp[n, pl.ds(ho, F, stride=H), :] = y[:, n * 128:n * 128 + 128]
            for n in range(3):
                bt[a, :, e * 384 + n * 128:e * 384 + n * 128 + 128] = tmp[n].astype(jnp.bfloat16)

def weights_call(w1, w2, aw):
    aw = aw.transpose(0, 3, 2, 1, 4).reshape(9, F, 3 * G)
    bf = lambda *s: jax.ShapeDtypeStruct(s, jnp.bfloat16)
    return pl.pallas_call(
        weights_kernel,
        out_shape=[bf(3, 256, 960), bf(192, 960), bf(3, 256, 960), bf(192, 960), bf(3, F * H, 3 * 384)],
        scratch_shapes=[pltpu.VMEM((3, F * H, 128), jnp.float32)],
        compiler_params=pltpu.CompilerParams(vmem_limit_bytes=32 * 2**20),
        cost_estimate=pl.CostEstimate(flops=10_000_000, bytes_accessed=10_000_000, transcendentals=0),
        name="pack_weights",
    )(w1.reshape(9, C, C), w2.reshape(9, C, C), aw)

FULL, PAIR = 480, 320
LP = 2 * 272 + REM

def cut(dst, at, src, start, m, rem):
    for n in range(2):
        dst[at + n * m:at + n * m + m, :] = src[n, pl.ds(start, m), :].astype(jnp.bfloat16)
    lane = lax.broadcasted_iota(jnp.int32, (rem, 128), 1)
    pair = jnp.where(lane < 64, src[2, pl.ds(start, rem), :], pltpu.roll(src[2, pl.ds(start + m - rem, rem), :], 64, 1))
    dst[at + 2 * m:at + 2 * m + rem, :] = pair.astype(jnp.bfloat16)

def uncut(dst, src, at, m, rem):
    for n in range(2):
        dst[n, 0:m, :] = src[at + n * m:at + n * m + m, :].astype(jnp.float32)
    x = src[at + 2 * m:at + 2 * m + rem, :].astype(jnp.float32)
    dst[2, 0:rem, :] = x
    dst[2, m - rem:m, :] = pltpu.roll(x, 64, 1)

def window_start(k):
    return 181 - BD * k

def pack_kernel(k_ref, lt, rt, before, after, full, up, down, far, lext, rext):
    k = k_ref[0]
    f32 = lambda x: x.astype(jnp.float32)
    for n in range(3):
        w = 128 if n < 2 else 64
        col = slice(n * 128, n * 128 + w)
        lext[n, 0:16, :w] = f32(before[0:16, col])
        lext[n, 16:272, :w] = f32(lt[:, col])
        lext[n, 272:288, :w] = f32(after[0:16, col])
        rext[n, 0:208, :w] = f32(before[16:224, col])
        rext[n, 208:464, :w] = f32(rt[:, col])
        rext[n, 464:480, :w] = f32(after[16:32, col])
    for dst in (full, up, down, far):
        cut(dst, 0, lext, 13, 272, REM)
    cut(full, LP, rext, 0, FULL, FULL // 2)
    cut(up, LP, rext, window_start((k + 2) & 7), 288, REM)
    cut(down, LP, rext, window_start((k + 6) & 7), 288, REM)
    cut(far, LP, rext, window_start(((k + 4) & 7) | 1), PAIR, PAIR // 2)

def relay_kernel(k_ref, got, up, down, rext):
    k = k_ref[0]
    uncut(rext, got, LP, FULL, FULL // 2)
    for dst, to in ((up, (k + 2) & 7), (down, (k + 6) & 7)):
        dst[0:LP, :] = got[0:LP, :]
        cut(dst, LP, rext, window_start(to), 288, REM)

def rows_of(n):
    return jax.ShapeDtypeStruct((n, 128), jnp.bfloat16)

EXACT, WHOLE, TWO = LP + 720, LP + 1200, LP + 800

def small_call(kernel, k, args, outs, scratch, name):
    return pl.pallas_call(
        kernel,
        out_shape=[rows_of(n) for n in outs],
        in_specs=[pl.BlockSpec(memory_space=pltpu.SMEM)] + [pl.BlockSpec(memory_space=pltpu.VMEM)] * len(args),
        scratch_shapes=[pltpu.VMEM((3, n, 128), jnp.float32) for n in scratch],
        compiler_params=pltpu.CompilerParams(vmem_limit_bytes=32 * 2**20),
        cost_estimate=pl.CostEstimate(flops=2_000_000, bytes_accessed=3_000_000, transcendentals=0),
        name=name,
    )(k, *args)

def corr2(l_ref, r_ref, v_ref, p):
    def tile(i, c):
        row = pl.multiple_of(i * 8, 8)
        q = [[None] * 5 for _ in range(2)]
        for m in range(4):
            for n in range(5):
                lt = l_ref[m * 5 + n, pl.ds(row, 8), :]
                for u in range(2):
                    pr = lt * r_ref[m * 5 + n, pl.ds(row + (25 - u) - 2 * p, 8), :]
                    q[u][n] = pr if m == 0 else q[u][n] + pr
        for u in range(2):
            x = jnp.concatenate(q[u], axis=1)
            x = x + pltpu.roll(x, 320, 1)
            for n in range(3):
                v_ref[u, n, pl.ds(row, 8), :] = x[:, n * 128:n * 128 + 128]
        return c
    lax.fori_loop(0, 33, tile, 0, unroll=3)

def agg_kernel(k_ref, l_ref, r_ref, b_ref, out_ref, lf_ref, rf_ref, v_ref, vs_ref):
    k = k_ref[0]
    for n in range(20):
        lf_ref[n] = l_ref[:, n * 128:n * 128 + 128].astype(jnp.float32)
        rf_ref[n, 0:MR, :] = r_ref[:, n * 128:n * 128 + 128].astype(jnp.float32)
    def pair(p, c):
        corr2(lf_ref, rf_ref, v_ref, p)
        for u in range(2):
            t = 2 * p + u
            d = 24 * k - 1 + t
            ok = jnp.logical_and(d >= 0, d < D)
            m = jnp.where(ok, 1.0, 0.0).astype(jnp.float32)
            for e in range(3):
                for n in range(3):
                    vs_ref[t, :, e * 384 + n * 128:e * 384 + n * 128 + 128] = (v_ref[u, n, e:e + WL, :] * m).astype(jnp.bfloat16)
        return c
    lax.fori_loop(0, NT // 2, pair, 0)
    def out(d, c):
        y = dot_nt(vs_ref[d], b_ref[0])
        y += dot_nt(vs_ref[d + 1], b_ref[1])
        y += dot_nt(vs_ref[d + 2], b_ref[2])
        y = jnp.maximum(y, 0.0).T.reshape(F, H, WL)
        out_ref[:, d] = y.astype(jnp.bfloat16)
        return c
    lax.fori_loop(0, BD, out, 0)

def agg_call(k, lx, rx, b):
    return pl.pallas_call(
        agg_kernel,
        out_shape=jax.ShapeDtypeStruct((F, BD, H, WL), jnp.bfloat16),
        in_specs=[pl.BlockSpec(memory_space=pltpu.SMEM)] + [pl.BlockSpec(memory_space=pltpu.VMEM)] * 3,
        out_specs=pl.BlockSpec(memory_space=pltpu.VMEM),
        scratch_shapes=[pltpu.VMEM((20, LR, 128), jnp.float32), pltpu.VMEM((20, RR, 128), jnp.float32),
                        pltpu.VMEM((2, 3, LR, 128), jnp.float32), pltpu.VMEM((NT, WL, KT), jnp.bfloat16)],
        compiler_params=pltpu.CompilerParams(vmem_limit_bytes=56 * 2**20),
        name="correlate_aggregate",
    )(k, lx, rx, b)


def from_col(x, by):
    n = lax.axis_size("col")
    return lax.ppermute(x, "col", [(i, i + by) for i in range(n) if 0 <= i + by < n])


def to_band(x, z, y):
    n = lax.axis_size("band")
    return lax.ppermute(x, "band", [(i, ((i + 2 * z) % n) ^ y) for i in range(n)])


def shards(left_view, right_view, first_weight, second_weight, agg_weight):
    k = lax.axis_index("band").astype(jnp.int32)
    base = lax.axis_index("col").astype(jnp.int32) * WL
    left = left_view[:, 0].T
    right = right_view[:, 0].T
    before = from_col(jnp.concatenate([left[WL - 16:], right[WL - 208:]], axis=0), 1)
    after = from_col(jnp.concatenate([left[:16], right[:16]], axis=0), -1)
    full, up, down, far = small_call(pack_kernel, k[None], (left, right, before, after), (WHOLE, EXACT, EXACT, TWO), (288, FULL), "pack_rows")
    across = to_band(full, 0, 1)
    above, below, twice = to_band(up, 1, 0), to_band(down, 3, 0), to_band(far, 2, 0)
    up, down = small_call(relay_kernel, k[None], (across,), (EXACT, EXACT), (FULL,), "relay_rows")
    rows = [full, across, above, below, twice, to_band(up, 1, 0), to_band(down, 3, 0), to_band(twice, 0, 1)]
    *weights, taps = weights_call(first_weight, second_weight, agg_weight)
    weights = (*weights, order_matrix())
    lf = conv_call(ML, 0, jnp.stack([k, base - 3]), rows, weights)
    rf = conv_call(MR, LP, jnp.stack([k, base - BD * k - 27]), rows, weights)
    return agg_call(k[None], lf, rf, taps)


def solution(mesh):
    return jax.shard_map(
        shards,
        mesh=mesh,
        in_specs=(P(None, "band", "col"), P(None, "band", "col"), P(), P(), P()),
        out_specs=P(None, "band", None, "col"),
        check_vma=False,
    )
```

```python
import functools

import jax
import jax.numpy as jnp
import numpy as np
from jax import lax
from jax.experimental import pallas as pl
from jax.experimental.pallas import tpu as pltpu
from jax.sharding import PartitionSpec as P

G, J, D, F, H, WL, BD, C, W = 40, 8, 192, 32, 8, 256, 24, 320, 4096
CH = J * H * G
REM = 144
ML, MR = 272, 288
LR, RR = 272, 296
NT = BD + 2
KT = 1024
UN = 4

def dot(x, w):
    return jnp.dot(x, w, preferred_element_type=jnp.float32)

def dot_on(x, i, y, j):
    return lax.dot_general(x, y, (((i,), (j,)), ((), ())), preferred_element_type=jnp.float32)

def build(dst, slot, src, m):
    for n in range(2):
        for e in range(3):
            dst[slot, :, (n * 3 + e) * 128:(n * 3 + e + 1) * 128] = src(n, e).astype(jnp.bfloat16)
    lane = lax.broadcasted_iota(jnp.int32, (m, 128), 1)
    pair = jnp.where(lane < 64, src(2, 0), pltpu.roll(src(2, 1), 64, 1))
    dst[slot, :, 768:896] = pair.astype(jnp.bfloat16)
    dst[slot, :, 896:960] = src(2, 2)[:, :64].astype(jnp.bfloat16)

def conv_kernel(m, at, s_ref, *refs):
    xin = refs[:8]
    wm1, wr1, wm2, wr2, out_ref, raw, xs, hs, ts, z, feat, wide = refs[8:]
    k, base = s_ref[0], s_ref[1]
    y = k & 1
    if at:
        start = window_start(k)
        formats = [(FULL, start)] * 2 + [(288, 0)] * 2 + [(PAIR, 24 - 24 * y), (288, 0), (288, 0), (PAIR, 24 - 24 * y)]
    else:
        formats = [(m, 0)] * 8
    source = [k, k ^ 1, (k + 6) & 7, (k + 2) & 7, (k + 4) & 7, ((k + 6) & 7) ^ 1, ((k + 2) & 7) ^ 1, ((k + 4) & 7) ^ 1]
    for d in range(8):
        h, (size, start) = source[d], formats[d]
        rem = REM if size == m else size // 2
        if size == m:
            uncut(raw.at[h], xin[d], at, m, rem)
        else:
            uncut(wide, xin[d], at, size, rem)
            for n in range(3):
                raw[h, n, 0:m, :] = wide[n, pl.ds(start, m), :]
    for slot in (0, 9):
        xs[slot] = jnp.zeros((m, 960), jnp.bfloat16)
        hs[slot] = jnp.zeros((m, 960), jnp.bfloat16)
        z[slot] = jnp.zeros((2, m, 128), jnp.float32)
    col = base + lax.broadcasted_iota(jnp.int32, (m, 128), 0)

    def rest(x, wr, h):
        y = dot(x[h + 1], wr[...])
        z[h + 1, 0] = y[:, :128]
        z[h + 1, 1, :, 0:64] = y[:, 128:192]

    def conv(x, wm, h):
        y = dot(x[h], wm[0])
        y += dot(x[h + 1], wm[1])
        y += dot(x[h + 2], wm[2])
        return y[:, :128], y[:, 128:], z[h, 0] + pltpu.roll(z[h + 1, 0], 64, 1) + z[h + 2, 1]

    def load(h, c):
        build(xs, h + 1, lambda n, e: raw[h, n, e:e + m, :], m)
        rest(xs, wr1, h)
        return c
    lax.fori_loop(0, H, load, 0, unroll=UN)
    def first(i, c):
        for u in range(UN):
            first_row(UN * i + u, ts.at[u])
        return c
    def first_row(h, ts):
        ok = jnp.logical_and(col + 1 >= 0, col + 1 < W)
        for n, y in enumerate(conv(xs, wm1, h)):
            ts[n, 0:m, :] = jnp.where(ok, jnp.maximum(y, 0.0), 0.0)
        build(hs, h + 1, lambda n, e: ts[n, e:e + m, :], m)
    lax.fori_loop(0, H // UN, first, 0)
    def rest2(h, c):
        rest(hs, wr2, h)
        return c
    lax.fori_loop(0, H, rest2, 0, unroll=UN)
    def second(h, c):
        ok = jnp.logical_and(col + 2 >= 0, col + 2 < W)
        for n, y in enumerate(conv(hs, wm2, h)):
            y = jnp.where(ok, y + raw[h, n, 2:2 + m, :], 0.0)
            feat[h, n] = y.astype(jnp.bfloat16).astype(jnp.float32)
        return c
    lax.fori_loop(0, H, second, 0, unroll=UN)

    lane = lax.broadcasted_iota(jnp.int32, (16, 128), 1)
    def place(i, c):
        row = pl.multiple_of(i * 16, 16)
        for q in range(20):
            got = None
            for j in range(J):
                for h in range(H):
                    t0 = j * H * G + h * G
                    lo, hi = max(t0, q * 128), min(t0 + G, q * 128 + 128)
                    if lo >= hi:
                        continue
                    s_lo = lo - t0 + j * G
                    while lo < hi:
                        n = s_lo // 128
                        length = min(hi - lo, (n + 1) * 128 - s_lo)
                        x = feat[h, n, pl.ds(row, 16), :]
                        sh = (lo - s_lo) % 128
                        if sh:
                            x = pltpu.roll(x, sh, 1)
                        got = x if got is None else jnp.where(lane >= lo - q * 128, x, got)
                        lo, s_lo = lo + length, s_lo + length
            out_ref[pl.ds(row, 16), q * 128:q * 128 + 128] = got.astype(jnp.bfloat16)
        return c
    lax.fori_loop(0, m // 16, place, 0, unroll=2)

def conv_call(m, at, scal, xs, weights):
    return pl.pallas_call(
        functools.partial(conv_kernel, m, at),
        out_shape=jax.ShapeDtypeStruct((m, CH), jnp.bfloat16),
        in_specs=[pl.BlockSpec(memory_space=pltpu.SMEM)] + [pl.BlockSpec(memory_space=pltpu.VMEM)] * 12,
        out_specs=pl.BlockSpec(memory_space=pltpu.VMEM),
        scratch_shapes=[pltpu.VMEM((8, 3, m + 8, 128), jnp.float32), pltpu.VMEM((10, m, 960), jnp.bfloat16),
                        pltpu.VMEM((10, m, 960), jnp.bfloat16), pltpu.VMEM((UN, 3, m + 8, 128), jnp.float32),
                        pltpu.VMEM((10, 2, m, 128), jnp.float32), pltpu.VMEM((8, 3, m, 128), jnp.float32), pltpu.VMEM((3, 480, 128), jnp.float32)],
        compiler_params=pltpu.CompilerParams(vmem_limit_bytes=56 * 2**20),
        cost_estimate=pl.CostEstimate(flops=2 * 18 * m * H * C * C * 2, bytes_accessed=6_000_000, transcendentals=0),
        name="feature_block",
    )(scal, *xs, *weights)

def order_matrix():
    to = np.arange(C)
    return jnp.asarray(np.arange(C)[:, None] == ((to % G) * J + to // G)[None, :], jnp.bfloat16)

def weights_kernel(w1, w2, aw, order, wm1, wr1, wm2, wr2, bt, tmp):
    lane = lax.broadcasted_iota(jnp.int32, (C, 128), 1)
    zero = jnp.zeros((C, 64), jnp.float32)
    for e in range(3):
        places = ((0, 128, e * 128), (128, 128, (3 + e) * 128), (256, 64, 768 + e * 64))
        for w, wm, wr, first in ((w1, wm1, wr1, True), (w2, wm2, wr2, False)):
            last = []
            for b in range(3):
                x = w[b * 3 + e]
                x = dot_on(order[...], 0, x, 1) if first else dot_on(x, 0, order[...], 0)
                for at, n, to in places:
                    wm[b, to:to + n, :] = x[at:at + n, :256].astype(jnp.bfloat16)
                last.append(jnp.concatenate([x[:, 256:320], zero], axis=1))
            pair = jnp.where(lane < 64, last[0], pltpu.roll(last[1], 64, 1)).astype(jnp.bfloat16)
            for at, n, to in places:
                wr[to:to + n, 0:128] = pair[at:at + n]
                wr[to:to + n, 128:192] = last[2][at:at + n, :64].astype(jnp.bfloat16)
    wide = lax.broadcasted_iota(jnp.int32, (F, 384), 1)
    for a in range(3):
        for e in range(3):
            x = jnp.concatenate([aw[a * 3 + e].astype(jnp.float32), jnp.zeros((F, 264), jnp.float32)], axis=1) * 0.125
            for ho in range(H):
                y = x if ho == 1 else pltpu.roll(x, ((ho - 1) * G) % 384, 1)
                y = jnp.where(wide < H * G, y, 0.0)
                for n in range(3):
                    tmp[n, pl.ds(ho, F, stride=H), :] = y[:, n * 128:n * 128 + 128]
            for n in range(2):
                at = a * KT + (n * 3 + e) * 128
                bt[at:at + 128, :] = tmp[n].T.astype(jnp.bfloat16)
            at, n = a * KT + 768 + e * 64, 64 if e < 2 else 128
            bt[at:at + n, :] = tmp[2].T[:n].astype(jnp.bfloat16)

def weights_call(w1, w2, aw, order):
    aw = aw.transpose(0, 3, 2, 1, 4).reshape(9, F, 3 * G)
    bf = lambda *s: jax.ShapeDtypeStruct(s, jnp.bfloat16)
    return pl.pallas_call(
        weights_kernel,
        out_shape=[bf(3, 960, 256), bf(960, 192), bf(3, 960, 256), bf(960, 192), bf(3 * KT, F * H)],
        scratch_shapes=[pltpu.VMEM((3, F * H, 128), jnp.float32)],
        compiler_params=pltpu.CompilerParams(vmem_limit_bytes=32 * 2**20),
        cost_estimate=pl.CostEstimate(flops=10_000_000, bytes_accessed=10_000_000, transcendentals=0),
        name="pack_weights",
    )(w1.reshape(9, C, C), w2.reshape(9, C, C), aw, order)

FULL, PAIR = 480, 320
LP = 2 * 272 + REM

def cut(dst, at, src, start, m, rem):
    for n in range(2):
        dst[at + n * m:at + n * m + m, :] = src[n, pl.ds(start, m), :].astype(jnp.bfloat16)
    lane = lax.broadcasted_iota(jnp.int32, (rem, 128), 1)
    pair = jnp.where(lane < 64, src[2, pl.ds(start, rem), :], pltpu.roll(src[2, pl.ds(start + m - rem, rem), :], 64, 1))
    dst[at + 2 * m:at + 2 * m + rem, :] = pair.astype(jnp.bfloat16)

def uncut(dst, src, at, m, rem):
    for n in range(2):
        dst[n, 0:m, :] = src[at + n * m:at + n * m + m, :].astype(jnp.float32)
    x = src[at + 2 * m:at + 2 * m + rem, :].astype(jnp.float32)
    dst[2, 0:rem, :] = x
    dst[2, m - rem:m, :] = pltpu.roll(x, 64, 1)

def window_start(k):
    return 181 - BD * k

def pack_kernel(k_ref, lt, rt, before, after, full, up, down, far, lext, rext):
    k = k_ref[0]
    f32 = lambda x: x.astype(jnp.float32)
    for n in range(3):
        w = 128 if n < 2 else 64
        col = slice(n * 128, n * 128 + w)
        lext[n, 0:16, :w] = f32(before[0:16, col])
        lext[n, 16:272, :w] = f32(lt[:, col])
        lext[n, 272:288, :w] = f32(after[0:16, col])
        rext[n, 0:208, :w] = f32(before[16:224, col])
        rext[n, 208:464, :w] = f32(rt[:, col])
        rext[n, 464:480, :w] = f32(after[16:32, col])
    for dst in (full, up, down, far):
        cut(dst, 0, lext, 13, 272, REM)
    cut(full, LP, rext, 0, FULL, FULL // 2)
    cut(up, LP, rext, window_start((k + 2) & 7), 288, REM)
    cut(down, LP, rext, window_start((k + 6) & 7), 288, REM)
    cut(far, LP, rext, window_start(((k + 4) & 7) | 1), PAIR, PAIR // 2)

def relay_kernel(k_ref, got, up, down, rext):
    k = k_ref[0]
    uncut(rext, got, LP, FULL, FULL // 2)
    for dst, to in ((up, (k + 2) & 7), (down, (k + 6) & 7)):
        dst[0:LP, :] = got[0:LP, :]
        cut(dst, LP, rext, window_start(to), 288, REM)

def rows_of(n):
    return jax.ShapeDtypeStruct((n, 128), jnp.bfloat16)

EXACT, WHOLE, TWO = LP + 720, LP + 1200, LP + 800

def small_call(kernel, k, args, outs, scratch, name):
    return pl.pallas_call(
        kernel,
        out_shape=[rows_of(n) for n in outs],
        in_specs=[pl.BlockSpec(memory_space=pltpu.SMEM)] + [pl.BlockSpec(memory_space=pltpu.VMEM)] * len(args),
        scratch_shapes=[pltpu.VMEM((3, n, 128), jnp.float32) for n in scratch],
        compiler_params=pltpu.CompilerParams(vmem_limit_bytes=32 * 2**20),
        cost_estimate=pl.CostEstimate(flops=2_000_000, bytes_accessed=3_000_000, transcendentals=0),
        name=name,
    )(k, *args)

def corr2(l_ref, r_ref, v_ref, p):
    def tile(i, c):
        row = pl.multiple_of(i * 8, 8)
        q = [[None] * 5 for _ in range(2)]
        for m in range(4):
            for n in range(5):
                lt = l_ref[m * 5 + n, pl.ds(row, 8), :]
                for u in range(2):
                    pr = lt * r_ref[m * 5 + n, pl.ds(row + (25 - u) - 2 * p, 8), :]
                    q[u][n] = pr if m == 0 else q[u][n] + pr
        for u in range(2):
            x = jnp.concatenate(q[u], axis=1)
            x = x + pltpu.roll(x, 320, 1)
            for n in range(3):
                v_ref[u, n, pl.ds(row, 8), :] = x[:, n * 128:n * 128 + 128]
        return c
    lax.fori_loop(0, 33, tile, 0, unroll=33)

def agg_kernel(k_ref, l_ref, r_ref, b_ref, out_ref, lf_ref, rf_ref, v_ref, vs0, vs1, vs2):
    k = k_ref[0]
    for n in range(20):
        lf_ref[n] = l_ref[:, n * 128:n * 128 + 128].astype(jnp.float32)
        rf_ref[n, 0:288, :] = r_ref[:, n * 128:n * 128 + 128].astype(jnp.float32)
    wide = lax.broadcasted_iota(jnp.int32, (WL, 128), 1)
    def pair(p, dst):
        corr2(lf_ref, rf_ref, v_ref, p)
        for u in range(2):
            def put(i, x, u=u):
                dst[:, u * KT + i * 128:u * KT + i * 128 + 128] = x.astype(jnp.bfloat16)
            for n in range(2):
                for e in range(3):
                    put(n * 3 + e, v_ref[u, n, e:e + WL, :])
            put(6, jnp.where(wide < 64, v_ref[u, 2, 0:WL, :], pltpu.roll(v_ref[u, 2, 1:1 + WL, :], 64, 1)))
            put(7, v_ref[u, 2, 2:2 + WL, :])
    def out(q, lo, hi):
        for u in range(2):
            if u == 0:
                y = jnp.dot(lo[...], b_ref[0:2 * KT], preferred_element_type=jnp.float32)
                y += jnp.dot(hi[:, 0:KT], b_ref[2 * KT:], preferred_element_type=jnp.float32)
            else:
                y = jnp.dot(lo[:, KT:], b_ref[0:KT], preferred_element_type=jnp.float32)
                y += jnp.dot(hi[...], b_ref[KT:], preferred_element_type=jnp.float32)
            y = jnp.maximum(y, 0.0).T.reshape(F, H, WL)
            out_ref[:, jnp.maximum(2 * q + u, 0)] = y.astype(jnp.bfloat16)
    bufs = (vs0, vs1, vs2)
    pair(0, vs0)
    @pl.when(k == 0)
    def _():
        vs0[:, 0:KT] = jnp.zeros((WL, KT), jnp.bfloat16)
    def three(i, c):
        for r in range(3):
            p = 1 + 3 * i + r
            new, lo, hi = bufs[(1 + r) % 3], bufs[(2 + r) % 3], bufs[r]
            out(p - 2, lo, hi)
            pair(p, new)
        return c
    lax.fori_loop(0, 4, three, 0)
    @pl.when(k == 7)
    def _():
        vs0[:, KT:] = jnp.zeros((WL, KT), jnp.bfloat16)
    out(11, vs2, vs0)

def agg_call(k, lx, rx, b):
    return pl.pallas_call(
        agg_kernel,
        out_shape=jax.ShapeDtypeStruct((F, BD, H, WL), jnp.bfloat16),
        in_specs=[pl.BlockSpec(memory_space=pltpu.SMEM)] + [pl.BlockSpec(memory_space=pltpu.VMEM)] * 3,
        out_specs=pl.BlockSpec(memory_space=pltpu.VMEM),
        scratch_shapes=[pltpu.VMEM((20, LR, 128), jnp.float32), pltpu.VMEM((20, RR, 128), jnp.float32),
                        pltpu.VMEM((2, 3, LR, 128), jnp.float32), *[pltpu.VMEM((WL, 2 * KT), jnp.bfloat16)] * 3],
        compiler_params=pltpu.CompilerParams(vmem_limit_bytes=56 * 2**20),
        name="correlate_aggregate",
    )(k, lx, rx, b)


def from_col(x, by):
    n = lax.axis_size("col")
    return lax.ppermute(x, "col", [(i, i + by) for i in range(n) if 0 <= i + by < n])


def to_band(x, z, y):
    n = lax.axis_size("band")
    return lax.ppermute(x, "band", [(i, ((i + 2 * z) % n) ^ y) for i in range(n)])


def shards(left_view, right_view, first_weight, second_weight, agg_weight):
    k = lax.axis_index("band").astype(jnp.int32)
    base = lax.axis_index("col").astype(jnp.int32) * WL
    order = order_matrix()
    left = dot_on(left_view[:, 0], 0, order, 0).astype(jnp.bfloat16)
    right = dot_on(right_view[:, 0], 0, order, 0).astype(jnp.bfloat16)
    before = from_col(jnp.concatenate([left[WL - 16:], right[WL - 208:]], axis=0), 1)
    after = from_col(jnp.concatenate([left[:16], right[:16]], axis=0), -1)
    full, up, down, far = small_call(pack_kernel, k[None], (left, right, before, after), (WHOLE, EXACT, EXACT, TWO), (288, FULL), "pack_rows")
    across = to_band(full, 0, 1)
    above, below, twice = to_band(up, 1, 0), to_band(down, 3, 0), to_band(far, 2, 0)
    up, down = small_call(relay_kernel, k[None], (across,), (EXACT, EXACT), (FULL,), "relay_rows")
    rows = [full, across, above, below, twice, to_band(up, 1, 0), to_band(down, 3, 0), to_band(twice, 0, 1)]
    *weights, taps = weights_call(first_weight, second_weight, agg_weight, order)
    lf = conv_call(ML, 0, jnp.stack([k, base - 3]), rows, weights)
    rf = conv_call(MR, LP, jnp.stack([k, base - BD * k - 27]), rows, weights)
    return agg_call(k[None], lf, rf, taps)


def solution(mesh):
    return jax.shard_map(
        shards,
        mesh=mesh,
        in_specs=(P(None, "band", "col"), P(None, "band", "col"), P(), P(), P()),
        out_specs=P(None, "band", None, "col"),
        check_vma=False,
    )
```

```python
import functools

import jax
import jax.numpy as jnp
import numpy as np
from jax import lax
from jax.experimental import pallas as pl
from jax.experimental.pallas import tpu as pltpu
from jax.sharding import PartitionSpec as P

G, J, D, F, H, WL, BD, C, W = 40, 8, 192, 32, 8, 256, 24, 320, 4096
CH = J * H * G
REM = 144
ML, MR = 272, 288
LR, RR = 272, 296
NT = BD + 2
KT = 1024
UN = 4


def dot(x, w):
    return jnp.dot(x, w, preferred_element_type=jnp.float32)


def dot_on(x, i, y, j):
    return lax.dot_general(x, y, (((i,), (j,)), ((), ())), preferred_element_type=jnp.float32)


def build(dst, slot, src, m):
    for n in range(2):
        for e in range(3):
            dst[slot, :, (n * 3 + e) * 128:(n * 3 + e + 1) * 128] = src(n, e).astype(jnp.bfloat16)
    lane = lax.broadcasted_iota(jnp.int32, (m, 128), 1)
    pair = jnp.where(lane < 64, src(2, 0), pltpu.roll(src(2, 1), 64, 1))
    dst[slot, :, 768:896] = pair.astype(jnp.bfloat16)
    dst[slot, :, 896:960] = src(2, 2)[:, :64].astype(jnp.bfloat16)


def feature_view(m, at, k, base, xin, wm1, wr1, wm2, wr2, target, raw, xs, hs, ts, z, feat, wide):
    y = k & 1
    if at:
        start = window_start(k)
        formats = [(FULL, start)] * 2 + [(288, 0)] * 2 + [(PAIR, 24 - 24 * y), (288, 0), (288, 0), (PAIR, 24 - 24 * y)]
    else:
        formats = [(m, 0)] * 8
    source = [k, k ^ 1, (k + 6) & 7, (k + 2) & 7, (k + 4) & 7, ((k + 6) & 7) ^ 1, ((k + 2) & 7) ^ 1, ((k + 4) & 7) ^ 1]
    for d in range(8):
        h, (size, start) = source[d], formats[d]
        rem = REM if size == m else size // 2
        if size == m:
            uncut(raw.at[h], xin[d], at, m, rem)
        else:
            uncut(wide, xin[d], at, size, rem)
            for n in range(3):
                raw[h, n, 0:m, :] = wide[n, pl.ds(start, m), :]
    xs, hs, z, feat = xs.at[:, 0:m], hs.at[:, 0:m], z.at[:, :, 0:m], feat.at[:, :, 0:m]
    col = base + lax.broadcasted_iota(jnp.int32, (m, 128), 0)

    def rest(x, wr, h):
        y = dot(x[h + 1], wr[...])
        z[h + 1, 0] = y[:, :128]
        z[h + 1, 1, :, 0:64] = y[:, 128:192]

    def conv(x, wm, h):
        y = dot(x[h], wm[0])
        y += dot(x[h + 1], wm[1])
        y += dot(x[h + 2], wm[2])
        return y[:, :128], y[:, 128:], z[h, 0] + pltpu.roll(z[h + 1, 0], 64, 1) + z[h + 2, 1]

    def load(h, c):
        build(xs, h + 1, lambda n, e: raw[h, n, e:e + m, :], m)
        rest(xs, wr1, h)
        return c
    lax.fori_loop(0, H, load, 0, unroll=UN)
    def first(i, c):
        for u in range(UN):
            first_row(UN * i + u, ts.at[u])
        return c
    def first_row(h, ts):
        ok = jnp.logical_and(col + 1 >= 0, col + 1 < W)
        for n, y in enumerate(conv(xs, wm1, h)):
            ts[n, 0:m, :] = jnp.where(ok, jnp.maximum(y, 0.0), 0.0)
        build(hs, h + 1, lambda n, e: ts[n, e:e + m, :], m)
    lax.fori_loop(0, H // UN, first, 0)
    def rest2(h, c):
        rest(hs, wr2, h)
        return c
    lax.fori_loop(0, H, rest2, 0, unroll=UN)
    def second(h, c):
        ok = jnp.logical_and(col + 2 >= 0, col + 2 < W)
        for n, y in enumerate(conv(hs, wm2, h)):
            y = jnp.where(ok, y + raw[h, n, 2:2 + m, :], 0.0)
            feat[h, n] = y.astype(jnp.bfloat16).astype(jnp.float32)
        return c
    lax.fori_loop(0, H, second, 0, unroll=UN)

    lane = lax.broadcasted_iota(jnp.int32, (16, 128), 1)
    def place(i, c):
        row = pl.multiple_of(i * 16, 16)
        for q in range(20):
            got = None
            for j in range(J):
                for h in range(H):
                    t0 = j * H * G + h * G
                    lo, hi = max(t0, q * 128), min(t0 + G, q * 128 + 128)
                    if lo >= hi:
                        continue
                    s_lo = lo - t0 + j * G
                    while lo < hi:
                        n = s_lo // 128
                        length = min(hi - lo, (n + 1) * 128 - s_lo)
                        x = feat[h, n, pl.ds(row, 16), :]
                        sh = (lo - s_lo) % 128
                        if sh:
                            x = pltpu.roll(x, sh, 1)
                        got = x if got is None else jnp.where(lane >= lo - q * 128, x, got)
                        lo, s_lo = lo + length, s_lo + length
            target[q, pl.ds(row, 16), :] = got
        return c
    lax.fori_loop(0, m // 16, place, 0, unroll=2)


def corr2(l_ref, r_ref, v_ref, p):
    def tile(i, c):
        row = pl.multiple_of(i * 8, 8)
        q = [[None] * 5 for _ in range(2)]
        for m in range(4):
            for n in range(5):
                lt = l_ref[m * 5 + n, pl.ds(row, 8), :]
                for u in range(2):
                    pr = lt * r_ref[m * 5 + n, pl.ds(row + (25 - u) - 2 * p, 8), :]
                    q[u][n] = pr if m == 0 else q[u][n] + pr
        for u in range(2):
            x = jnp.concatenate(q[u], axis=1)
            x = x + pltpu.roll(x, 320, 1)
            for n in range(3):
                v_ref[u, n, pl.ds(row, 8), :] = x[:, n * 128:n * 128 + 128]
        return c
    lax.fori_loop(0, 33, tile, 0, unroll=33)


def aggregate_views(k, b_ref, out_ref, lf_ref, rf_ref, v_ref, vs0, vs1, vs2):
    wide = lax.broadcasted_iota(jnp.int32, (WL, 128), 1)
    def pair(p, dst):
        corr2(lf_ref, rf_ref, v_ref, p)
        for u in range(2):
            def put(i, x, u=u):
                dst[:, u * KT + i * 128:u * KT + i * 128 + 128] = x.astype(jnp.bfloat16)
            for n in range(2):
                for e in range(3):
                    put(n * 3 + e, v_ref[u, n, e:e + WL, :])
            put(6, jnp.where(wide < 64, v_ref[u, 2, 0:WL, :], pltpu.roll(v_ref[u, 2, 1:1 + WL, :], 64, 1)))
            put(7, v_ref[u, 2, 2:2 + WL, :])
    def out(q, lo, hi):
        for u in range(2):
            if u == 0:
                y = jnp.dot(lo[...], b_ref[0:2 * KT], preferred_element_type=jnp.float32)
                y += jnp.dot(hi[:, 0:KT], b_ref[2 * KT:], preferred_element_type=jnp.float32)
            else:
                y = jnp.dot(lo[:, KT:], b_ref[0:KT], preferred_element_type=jnp.float32)
                y += jnp.dot(hi[...], b_ref[KT:], preferred_element_type=jnp.float32)
            y = jnp.maximum(y, 0.0).T.reshape(F, H, WL)
            out_ref[:, jnp.maximum(2 * q + u, 0)] = y.astype(jnp.bfloat16)
    bufs = (vs0, vs1, vs2)
    pair(0, vs0)
    @pl.when(k == 0)
    def _():
        vs0[:, 0:KT] = jnp.zeros((WL, KT), jnp.bfloat16)
    def three(i, c):
        for r in range(3):
            p = 1 + 3 * i + r
            new, lo, hi = bufs[(1 + r) % 3], bufs[(2 + r) % 3], bufs[r]
            out(p - 2, lo, hi)
            pair(p, new)
        return c
    lax.fori_loop(0, 4, three, 0)
    @pl.when(k == 7)
    def _():
        vs0[:, KT:] = jnp.zeros((WL, KT), jnp.bfloat16)
    out(11, vs2, vs0)


def order_matrix():
    to = np.arange(C)
    return jnp.asarray(np.arange(C)[:, None] == ((to % G) * J + to // G)[None, :], jnp.bfloat16)


def weights_kernel(w1, w2, aw, order, wm1, wr1, wm2, wr2, bt, tmp):
    lane = lax.broadcasted_iota(jnp.int32, (C, 128), 1)
    zero = jnp.zeros((C, 64), jnp.float32)
    for e in range(3):
        places = ((0, 128, e * 128), (128, 128, (3 + e) * 128), (256, 64, 768 + e * 64))
        for w, wm, wr, first in ((w1, wm1, wr1, True), (w2, wm2, wr2, False)):
            last = []
            for b in range(3):
                x = w[b * 3 + e]
                x = dot_on(order[...], 0, x, 1) if first else dot_on(x, 0, order[...], 0)
                for at, n, to in places:
                    wm[b, to:to + n, :] = x[at:at + n, :256].astype(jnp.bfloat16)
                last.append(jnp.concatenate([x[:, 256:320], zero], axis=1))
            pair = jnp.where(lane < 64, last[0], pltpu.roll(last[1], 64, 1)).astype(jnp.bfloat16)
            for at, n, to in places:
                wr[to:to + n, 0:128] = pair[at:at + n]
                wr[to:to + n, 128:192] = last[2][at:at + n, :64].astype(jnp.bfloat16)
    wide = lax.broadcasted_iota(jnp.int32, (F, 384), 1)
    for a in range(3):
        for e in range(3):
            x = [aw[(a * 3 + b) * 3 + e].astype(jnp.float32) for b in range(3)]
            x = jnp.concatenate(x + [jnp.zeros((F, 264), jnp.float32)], axis=1) * 0.125
            for ho in range(H):
                y = x if ho == 1 else pltpu.roll(x, ((ho - 1) * G) % 384, 1)
                y = jnp.where(wide < H * G, y, 0.0)
                for n in range(3):
                    tmp[n, pl.ds(ho, F, stride=H), :] = y[:, n * 128:n * 128 + 128]
            for n in range(2):
                at = a * KT + (n * 3 + e) * 128
                bt[at:at + 128, :] = tmp[n].T.astype(jnp.bfloat16)
            at, n = a * KT + 768 + e * 64, 64 if e < 2 else 128
            bt[at:at + n, :] = tmp[2].T[:n].astype(jnp.bfloat16)


def weights_call(w1, w2, aw, order):
    aw = aw.transpose(0, 1, 3, 2, 4).reshape(27, F, G)
    bf = lambda *s: jax.ShapeDtypeStruct(s, jnp.bfloat16)
    return pl.pallas_call(
        weights_kernel,
        out_shape=[bf(3, 960, 256), bf(960, 192), bf(3, 960, 256), bf(960, 192), bf(3 * KT, F * H)],
        scratch_shapes=[pltpu.VMEM((3, F * H, 128), jnp.float32)],
        compiler_params=pltpu.CompilerParams(vmem_limit_bytes=56 * 2**20),
        cost_estimate=pl.CostEstimate(flops=10_000_000, bytes_accessed=10_000_000, transcendentals=0),
        name="pack_weights",
    )(w1.reshape(9, C, C), w2.reshape(9, C, C), aw, order)

FULL, PAIR = 480, 320
LP = 2 * 272 + REM


def cut(dst, at, src, start, m, rem):
    for n in range(2):
        dst[at + n * m:at + n * m + m, :] = src[n, pl.ds(start, m), :].astype(jnp.bfloat16)
    lane = lax.broadcasted_iota(jnp.int32, (rem, 128), 1)
    pair = jnp.where(lane < 64, src[2, pl.ds(start, rem), :], pltpu.roll(src[2, pl.ds(start + m - rem, rem), :], 64, 1))
    dst[at + 2 * m:at + 2 * m + rem, :] = pair.astype(jnp.bfloat16)


def uncut(dst, src, at, m, rem):
    for n in range(2):
        dst[n, 0:m, :] = src[at + n * m:at + n * m + m, :].astype(jnp.float32)
    x = src[at + 2 * m:at + 2 * m + rem, :].astype(jnp.float32)
    dst[2, 0:rem, :] = x
    dst[2, m - rem:m, :] = pltpu.roll(x, 64, 1)


def window_start(k):
    return 181 - BD * k


def pack_kernel(k_ref, lt, rt, before, after, full, up, down, far, lext, rext):
    k = k_ref[0]
    f32 = lambda x: x.astype(jnp.float32)
    for n in range(3):
        w = 128 if n < 2 else 64
        col = slice(n * 128, n * 128 + w)
        lext[n, 0:16, :w] = f32(before[0:16, col])
        lext[n, 16:272, :w] = f32(lt[:, col])
        lext[n, 272:288, :w] = f32(after[0:16, col])
        rext[n, 0:208, :w] = f32(before[16:224, col])
        rext[n, 208:464, :w] = f32(rt[:, col])
        rext[n, 464:480, :w] = f32(after[16:32, col])
    for dst in (full, up, down, far):
        cut(dst, 0, lext, 13, 272, REM)
    cut(full, LP, rext, 0, FULL, FULL // 2)
    cut(up, LP, rext, window_start((k + 2) & 7), 288, REM)
    cut(down, LP, rext, window_start((k + 6) & 7), 288, REM)
    cut(far, LP, rext, window_start(((k + 4) & 7) | 1), PAIR, PAIR // 2)


def relay_kernel(k_ref, got, up, down, rext):
    k = k_ref[0]
    uncut(rext, got, LP, FULL, FULL // 2)
    for dst, to in ((up, (k + 2) & 7), (down, (k + 6) & 7)):
        dst[0:LP, :] = got[0:LP, :]
        cut(dst, LP, rext, window_start(to), 288, REM)


def rows_of(n):
    return jax.ShapeDtypeStruct((n, 128), jnp.bfloat16)

EXACT, WHOLE, TWO = LP + 720, LP + 1200, LP + 800


def small_call(kernel, k, args, outs, scratch, name):
    return pl.pallas_call(
        kernel,
        out_shape=[rows_of(n) for n in outs],
        in_specs=[pl.BlockSpec(memory_space=pltpu.SMEM)] + [pl.BlockSpec(memory_space=pltpu.VMEM)] * len(args),
        scratch_shapes=[pltpu.VMEM((3, n, 128), jnp.float32) for n in scratch],
        compiler_params=pltpu.CompilerParams(vmem_limit_bytes=56 * 2**20),
        cost_estimate=pl.CostEstimate(flops=2_000_000, bytes_accessed=3_000_000, transcendentals=0),
        name=name,
    )(k, *args)


def main_kernel(s_ref, *refs):
    xin, (wm1, wr1, wm2, wr2, taps, out_ref), scratch = refs[:8], refs[8:14], refs[14:]
    conv_scratch, (lf, rf, *others) = scratch[:7], scratch[7:]
    k, base = s_ref[0], s_ref[1]
    raw, xs, hs, ts, z = conv_scratch[:5]
    for slot in (0, 9):
        xs[slot] = jnp.zeros((MR, 960), jnp.bfloat16)
        hs[slot] = jnp.zeros((MR, 960), jnp.bfloat16)
        z[slot] = jnp.zeros((2, MR, 128), jnp.float32)
    feature_view(ML, 0, k, base - 3, xin, wm1, wr1, wm2, wr2, lf, *conv_scratch)
    feature_view(MR, LP, k, base - BD * k - 27, xin, wm1, wr1, wm2, wr2, rf, *conv_scratch)
    aggregate_views(k, taps, out_ref, lf, rf, *others)


def main_call(scal, rows, weights, taps):
    f32 = lambda *s: pltpu.VMEM(s, jnp.float32)
    b16 = lambda *s: pltpu.VMEM(s, jnp.bfloat16)
    return pl.pallas_call(
        main_kernel,
        out_shape=jax.ShapeDtypeStruct((F, BD, H, WL), jnp.bfloat16),
        in_specs=[pl.BlockSpec(memory_space=pltpu.SMEM)] + [pl.BlockSpec(memory_space=pltpu.VMEM)] * 13,
        out_specs=pl.BlockSpec(memory_space=pltpu.VMEM),
        scratch_shapes=[f32(8, 3, MR + 8, 128), b16(10, MR, 960), b16(10, MR, 960), f32(UN, 3, MR + 8, 128), f32(10, 2, MR, 128),
                        f32(8, 3, MR, 128), f32(3, FULL, 128), f32(20, LR, 128), f32(20, RR, 128), f32(2, 3, LR, 128),
                        b16(WL, 2 * KT), b16(WL, 2 * KT), b16(WL, 2 * KT)],
        compiler_params=pltpu.CompilerParams(vmem_limit_bytes=60 * 2**20),
        name="features_volume_aggregate",
    )(scal, *rows, *weights, taps)


def from_col(x, by):
    n = lax.axis_size("col")
    return lax.ppermute(x, "col", [(i, i + by) for i in range(n) if 0 <= i + by < n])


def to_band(x, z, y):
    n = lax.axis_size("band")
    return lax.ppermute(x, "band", [(i, ((i + 2 * z) % n) ^ y) for i in range(n)])


def shards(left_view, right_view, first_weight, second_weight, agg_weight):
    k = lax.axis_index("band").astype(jnp.int32)
    base = lax.axis_index("col").astype(jnp.int32) * WL
    order = order_matrix()
    left = dot_on(left_view[:, 0], 0, order, 0).astype(jnp.bfloat16)
    right = dot_on(right_view[:, 0], 0, order, 0).astype(jnp.bfloat16)
    before = from_col(jnp.concatenate([left[WL - 16:], right[WL - 208:]], axis=0), 1)
    after = from_col(jnp.concatenate([left[:16], right[:16]], axis=0), -1)
    *weights, taps = weights_call(first_weight, second_weight, agg_weight, order)
    full, up, down, far = small_call(pack_kernel, k[None], (left, right, before, after), (WHOLE, EXACT, EXACT, TWO), (288, FULL), "pack_rows")
    across = to_band(full, 0, 1)
    above, below, twice = to_band(up, 1, 0), to_band(down, 3, 0), to_band(far, 2, 0)
    up, down = small_call(relay_kernel, k[None], (across,), (EXACT, EXACT), (FULL,), "relay_rows")
    rows = [full, across, above, below, twice, to_band(up, 1, 0), to_band(down, 3, 0), to_band(twice, 0, 1)]
    return main_call(jnp.stack([k, base]), rows, weights, taps)


def solution(mesh):
    return jax.shard_map(
        shards,
        mesh=mesh,
        in_specs=(P(None, "band", "col"), P(None, "band", "col"), P(), P(), P()),
        out_specs=P(None, "band", None, "col"),
        check_vma=False,
    )
```

```python
import functools

import jax
import jax.numpy as jnp
import numpy as np
from jax import lax
from jax.experimental import pallas as pl
from jax.experimental.pallas import tpu as pltpu
from jax.sharding import PartitionSpec as P

G, J, D, F, H, WL, BD, C, W = 40, 8, 192, 32, 8, 256, 24, 320, 4096
CH = J * H * G
REM = 144
ML, MR = 272, 288
LR, RR = 272, 296
NT = BD + 2
KT = 1024
UN = 8


def dot(x, w):
    return jnp.dot(x, w, preferred_element_type=jnp.float32)


def dot_on(x, i, y, j):
    return lax.dot_general(x, y, (((i,), (j,)), ((), ())), preferred_element_type=jnp.float32)


def build(dst, slot, src, m):
    for n in range(2):
        for e in range(3):
            dst[slot, :, (n * 3 + e) * 128:(n * 3 + e + 1) * 128] = src(n, e).astype(jnp.bfloat16)
    lane = lax.broadcasted_iota(jnp.int32, (m, 128), 1)
    pair = jnp.where(lane < 64, src(2, 0), pltpu.roll(src(2, 1), 64, 1))
    dst[slot, :, 768:896] = pair.astype(jnp.bfloat16)
    dst[slot, :, 896:960] = src(2, 2)[:, :64].astype(jnp.bfloat16)


def feature_view(m, at, k, base, xin, wm1, wr1, wm2, wr2, target, raw, xs, hs, ts, z, feat, wide):
    y = k & 1
    if at:
        start = window_start(k)
        formats = [(FULL, start)] * 2 + [(288, 0)] * 2 + [(PAIR, 24 - 24 * y), (288, 0), (288, 0), (PAIR, 24 - 24 * y)]
    else:
        formats = [(m, 0)] * 8
    source = [k, k ^ 1, (k + 6) & 7, (k + 2) & 7, (k + 4) & 7, ((k + 6) & 7) ^ 1, ((k + 2) & 7) ^ 1, ((k + 4) & 7) ^ 1]
    for d in range(8):
        h, (size, start) = source[d], formats[d]
        rem = REM if size == m else size // 2
        if size == m:
            uncut(raw.at[h], xin[d], at, m, rem)
        else:
            uncut(wide, xin[d], at, size, rem)
            for n in range(3):
                raw[h, n, 0:m, :] = wide[n, pl.ds(start, m), :]
    xs, hs, z, feat = xs.at[:, 0:m], hs.at[:, 0:m], z.at[:, :, 0:m], feat.at[:, :, 0:m]
    col = base + lax.broadcasted_iota(jnp.int32, (m, 128), 0)

    def rest(x, wr, h):
        y = dot(x[h + 1], wr[...])
        z[h + 1, 0] = y[:, :128]
        z[h + 1, 1, :, 0:64] = y[:, 128:192]

    def conv(x, wm, h):
        y = dot(x[h + 1], wm[1])
        if h > 0:
            y += dot(x[h], wm[0])
        if h < H - 1:
            y += dot(x[h + 2], wm[2])
        return y[:, :128], y[:, 128:], z[h, 0] + pltpu.roll(z[h + 1, 0], 64, 1) + z[h + 2, 1]

    def load(h, c):
        build(xs, h + 1, lambda n, e: raw[h, n, e:e + m, :], m)
        rest(xs, wr1, h)
        return c
    for h in range(H):
        load(h, 0)
    def first(i, c):
        for u in range(UN):
            first_row(UN * i + u, ts.at[u])
        return c
    def first_row(h, ts):
        ok = jnp.logical_and(col + 1 >= 0, col + 1 < W)
        for n, y in enumerate(conv(xs, wm1, h)):
            ts[n, 0:m, :] = jnp.where(ok, jnp.maximum(y, 0.0), 0.0)
        build(hs, h + 1, lambda n, e: ts[n, e:e + m, :], m)
    first(0, 0)
    def rest2(h, c):
        rest(hs, wr2, h)
        return c
    for h in range(H):
        rest2(h, 0)
    def second(h, c):
        ok = jnp.logical_and(col + 2 >= 0, col + 2 < W)
        for n, y in enumerate(conv(hs, wm2, h)):
            y = jnp.where(ok, y + raw[h, n, 2:2 + m, :], 0.0)
            feat[h, n] = y.astype(jnp.bfloat16).astype(jnp.float32)
        return c
    for h in range(H):
        second(h, 0)

    lane = lax.broadcasted_iota(jnp.int32, (16, 128), 1)
    def place(i, c):
        row = pl.multiple_of(i * 16, 16)
        for q in range(20):
            got = None
            for j in range(J):
                for h in range(H):
                    t0 = j * H * G + h * G
                    lo, hi = max(t0, q * 128), min(t0 + G, q * 128 + 128)
                    if lo >= hi:
                        continue
                    s_lo = lo - t0 + j * G
                    while lo < hi:
                        n = s_lo // 128
                        length = min(hi - lo, (n + 1) * 128 - s_lo)
                        x = feat[h, n, pl.ds(row, 16), :]
                        sh = (lo - s_lo) % 128
                        if sh:
                            x = pltpu.roll(x, sh, 1)
                        got = x if got is None else jnp.where(lane >= lo - q * 128, x, got)
                        lo, s_lo = lo + length, s_lo + length
            target[q, pl.ds(row, 16), :] = got
        return c
    lax.fori_loop(0, m // 16, place, 0, unroll=2)


def corr2(l_ref, r_ref, v_ref, p):
    def tile(i, c):
        row = pl.multiple_of(i * 8, 8)
        q = [[None] * 5 for _ in range(2)]
        for m in range(4):
            for n in range(5):
                lt = l_ref[m * 5 + n, pl.ds(row, 8), :]
                for u in range(2):
                    pr = lt * r_ref[m * 5 + n, pl.ds(row + (25 - u) - 2 * p, 8), :]
                    q[u][n] = pr if m == 0 else q[u][n] + pr
        for u in range(2):
            x = jnp.concatenate(q[u], axis=1)
            x = x + pltpu.roll(x, 320, 1)
            for n in range(3):
                v_ref[u, n, pl.ds(row, 8), :] = x[:, n * 128:n * 128 + 128]
        return c
    lax.fori_loop(0, 33, tile, 0, unroll=33)


def aggregate_views(k, b_ref, out_ref, lf_ref, rf_ref, v_ref, vs0, vs1, vs2):
    wide = lax.broadcasted_iota(jnp.int32, (WL, 128), 1)
    def pair(p, dst):
        corr2(lf_ref, rf_ref, v_ref, p)
        for u in range(2):
            def put(i, x, u=u):
                dst[:, u * KT + i * 128:u * KT + i * 128 + 128] = x.astype(jnp.bfloat16)
            for n in range(2):
                for e in range(3):
                    put(n * 3 + e, v_ref[u, n, e:e + WL, :])
            put(6, jnp.where(wide < 64, v_ref[u, 2, 0:WL, :], pltpu.roll(v_ref[u, 2, 1:1 + WL, :], 64, 1)))
            put(7, v_ref[u, 2, 2:2 + WL, :])
    def out(q, lo, hi):
        for u in range(2):
            if u == 0:
                y = jnp.dot(lo[...], b_ref[0:2 * KT], preferred_element_type=jnp.float32)
                y += jnp.dot(hi[:, 0:KT], b_ref[2 * KT:], preferred_element_type=jnp.float32)
            else:
                y = jnp.dot(lo[:, KT:], b_ref[0:KT], preferred_element_type=jnp.float32)
                y += jnp.dot(hi[...], b_ref[KT:], preferred_element_type=jnp.float32)
            y = jnp.maximum(y, 0.0).T.reshape(F, H, WL)
            out_ref[:, jnp.maximum(2 * q + u, 0)] = y.astype(jnp.bfloat16)
    bufs = (vs0, vs1, vs2)
    pair(0, vs0)
    @pl.when(k == 0)
    def _():
        vs0[:, 0:KT] = jnp.zeros((WL, KT), jnp.bfloat16)
    def three(i, c):
        for r in range(3):
            p = 1 + 3 * i + r
            new, lo, hi = bufs[(1 + r) % 3], bufs[(2 + r) % 3], bufs[r]
            out(p - 2, lo, hi)
            pair(p, new)
        return c
    lax.fori_loop(0, 4, three, 0)
    @pl.when(k == 7)
    def _():
        vs0[:, KT:] = jnp.zeros((WL, KT), jnp.bfloat16)
    out(11, vs2, vs0)


def order_matrix():
    to = np.arange(C)
    return jnp.asarray(np.arange(C)[:, None] == ((to % G) * J + to // G)[None, :], jnp.bfloat16)


def weights_kernel(w1, w2, aw, order, wm1, wr1, wm2, wr2, bt, tmp):
    lane = lax.broadcasted_iota(jnp.int32, (C, 128), 1)
    zero = jnp.zeros((C, 64), jnp.float32)
    for e in range(3):
        places = ((0, 128, e * 128), (128, 128, (3 + e) * 128), (256, 64, 768 + e * 64))
        for w, wm, wr, first in ((w1, wm1, wr1, True), (w2, wm2, wr2, False)):
            last = []
            for b in range(3):
                x = w[b * 3 + e]
                x = dot_on(order[...], 0, x, 1) if first else dot_on(x, 0, order[...], 0)
                for at, n, to in places:
                    wm[b, to:to + n, :] = x[at:at + n, :256].astype(jnp.bfloat16)
                last.append(jnp.concatenate([x[:, 256:320], zero], axis=1))
            pair = jnp.where(lane < 64, last[0], pltpu.roll(last[1], 64, 1)).astype(jnp.bfloat16)
            for at, n, to in places:
                wr[to:to + n, 0:128] = pair[at:at + n]
                wr[to:to + n, 128:192] = last[2][at:at + n, :64].astype(jnp.bfloat16)
    wide = lax.broadcasted_iota(jnp.int32, (F, 384), 1)
    for a in range(3):
        for e in range(3):
            x = [aw[(a * 3 + b) * 3 + e].astype(jnp.float32) for b in range(3)]
            x = jnp.concatenate(x + [jnp.zeros((F, 264), jnp.float32)], axis=1) * 0.125
            for ho in range(H):
                y = x if ho == 1 else pltpu.roll(x, ((ho - 1) * G) % 384, 1)
                y = jnp.where(wide < H * G, y, 0.0)
                for n in range(3):
                    tmp[n, pl.ds(ho, F, stride=H), :] = y[:, n * 128:n * 128 + 128]
            for n in range(2):
                at = a * KT + (n * 3 + e) * 128
                bt[at:at + 128, :] = tmp[n].T.astype(jnp.bfloat16)
            at, n = a * KT + 768 + e * 64, 64 if e < 2 else 128
            bt[at:at + n, :] = tmp[2].T[:n].astype(jnp.bfloat16)


def weights_call(w1, w2, aw, order):
    aw = aw.transpose(0, 1, 3, 2, 4).reshape(27, F, G)
    bf = lambda *s: jax.ShapeDtypeStruct(s, jnp.bfloat16)
    return pl.pallas_call(
        weights_kernel,
        out_shape=[bf(3, 960, 256), bf(960, 192), bf(3, 960, 256), bf(960, 192), bf(3 * KT, F * H)],
        scratch_shapes=[pltpu.VMEM((3, F * H, 128), jnp.float32)],
        compiler_params=pltpu.CompilerParams(vmem_limit_bytes=56 * 2**20),
        cost_estimate=pl.CostEstimate(flops=10_000_000, bytes_accessed=10_000_000, transcendentals=0),
        name="pack_weights",
    )(w1.reshape(9, C, C), w2.reshape(9, C, C), aw, order)

FULL, PAIR = 480, 320
LP = 2 * 272 + REM


def cut(dst, at, src, start, m, rem):
    for n in range(2):
        dst[at + n * m:at + n * m + m, :] = src[n, pl.ds(start, m), :].astype(jnp.bfloat16)
    lane = lax.broadcasted_iota(jnp.int32, (rem, 128), 1)
    pair = jnp.where(lane < 64, src[2, pl.ds(start, rem), :], pltpu.roll(src[2, pl.ds(start + m - rem, rem), :], 64, 1))
    dst[at + 2 * m:at + 2 * m + rem, :] = pair.astype(jnp.bfloat16)


def uncut(dst, src, at, m, rem):
    for n in range(2):
        dst[n, 0:m, :] = src[at + n * m:at + n * m + m, :].astype(jnp.float32)
    x = src[at + 2 * m:at + 2 * m + rem, :].astype(jnp.float32)
    dst[2, 0:rem, :] = x
    dst[2, m - rem:m, :] = pltpu.roll(x, 64, 1)


def window_start(k):
    return 181 - BD * k


def pack_kernel(k_ref, lt, rt, before, after, full, up, down, far, lext, rext):
    k = k_ref[0]
    f32 = lambda x: x.astype(jnp.float32)
    for n in range(3):
        w = 128 if n < 2 else 64
        col = slice(n * 128, n * 128 + w)
        lext[n, 0:16, :w] = f32(before[0:16, col])
        lext[n, 16:272, :w] = f32(lt[:, col])
        lext[n, 272:288, :w] = f32(after[0:16, col])
        rext[n, 0:208, :w] = f32(before[16:224, col])
        rext[n, 208:464, :w] = f32(rt[:, col])
        rext[n, 464:480, :w] = f32(after[16:32, col])
    for dst in (full, up, down, far):
        cut(dst, 0, lext, 13, 272, REM)
    cut(full, LP, rext, 0, FULL, FULL // 2)
    cut(up, LP, rext, window_start((k + 2) & 7), 288, REM)
    cut(down, LP, rext, window_start((k + 6) & 7), 288, REM)
    cut(far, LP, rext, window_start(((k + 4) & 7) | 1), PAIR, PAIR // 2)


def relay_kernel(k_ref, got, up, down, rext):
    k = k_ref[0]
    uncut(rext, got, LP, FULL, FULL // 2)
    for dst, to in ((up, (k + 2) & 7), (down, (k + 6) & 7)):
        dst[0:LP, :] = got[0:LP, :]
        cut(dst, LP, rext, window_start(to), 288, REM)


def rows_of(n):
    return jax.ShapeDtypeStruct((n, 128), jnp.bfloat16)

EXACT, WHOLE, TWO = LP + 720, LP + 1200, LP + 800


def small_call(kernel, k, args, outs, scratch, name):
    return pl.pallas_call(
        kernel,
        out_shape=[rows_of(n) for n in outs],
        in_specs=[pl.BlockSpec(memory_space=pltpu.SMEM)] + [pl.BlockSpec(memory_space=pltpu.VMEM)] * len(args),
        scratch_shapes=[pltpu.VMEM((3, n, 128), jnp.float32) for n in scratch],
        compiler_params=pltpu.CompilerParams(vmem_limit_bytes=32 * 2**20),
        cost_estimate=pl.CostEstimate(flops=2_000_000, bytes_accessed=3_000_000, transcendentals=0),
        name=name,
    )(k, *args)


def main_kernel(s_ref, *refs):
    xin, (wm1, wr1, wm2, wr2, taps, out_ref), scratch = refs[:8], refs[8:14], refs[14:]
    conv_scratch, (lf, rf, *others) = scratch[:7], scratch[7:]
    k, base = s_ref[0], s_ref[1]
    raw, xs, hs, ts, z = conv_scratch[:5]
    for slot in (0, 9):
        xs[slot] = jnp.zeros((MR, 960), jnp.bfloat16)
        hs[slot] = jnp.zeros((MR, 960), jnp.bfloat16)
        z[slot] = jnp.zeros((2, MR, 128), jnp.float32)
    feature_view(ML, 0, k, base - 3, xin, wm1, wr1, wm2, wr2, lf, *conv_scratch)
    feature_view(MR, LP, k, base - BD * k - 27, xin, wm1, wr1, wm2, wr2, rf, *conv_scratch)
    aggregate_views(k, taps, out_ref, lf, rf, *others)


def main_call(scal, rows, weights, taps):
    f32 = lambda *s: pltpu.VMEM(s, jnp.float32)
    b16 = lambda *s: pltpu.VMEM(s, jnp.bfloat16)
    return pl.pallas_call(
        main_kernel,
        out_shape=jax.ShapeDtypeStruct((F, BD, H, WL), jnp.bfloat16),
        in_specs=[pl.BlockSpec(memory_space=pltpu.SMEM)] + [pl.BlockSpec(memory_space=pltpu.VMEM)] * 13,
        out_specs=pl.BlockSpec(memory_space=pltpu.VMEM),
        scratch_shapes=[f32(8, 3, MR + 8, 128), b16(10, MR, 960), b16(10, MR, 960), f32(UN, 3, MR + 8, 128), f32(10, 2, MR, 128),
                        f32(8, 3, MR, 128), f32(3, FULL, 128), f32(20, LR, 128), f32(20, RR, 128), f32(2, 3, LR, 128),
                        b16(WL, 2 * KT), b16(WL, 2 * KT), b16(WL, 2 * KT)],
        compiler_params=pltpu.CompilerParams(vmem_limit_bytes=60 * 2**20),
        name="features_volume_aggregate",
    )(scal, *rows, *weights, taps)


def from_col(x, by):
    n = lax.axis_size("col")
    return lax.ppermute(x, "col", [(i, i + by) for i in range(n) if 0 <= i + by < n])


def to_band(x, z, y):
    n = lax.axis_size("band")
    return lax.ppermute(x, "band", [(i, ((i + 2 * z) % n) ^ y) for i in range(n)])


def shards(left_view, right_view, first_weight, second_weight, agg_weight):
    k = lax.axis_index("band").astype(jnp.int32)
    base = lax.axis_index("col").astype(jnp.int32) * WL
    order = order_matrix()
    left = dot_on(left_view[:, 0], 0, order, 0).astype(jnp.bfloat16)
    right = dot_on(right_view[:, 0], 0, order, 0).astype(jnp.bfloat16)
    before = from_col(jnp.concatenate([left[WL - 16:], right[WL - 208:]], axis=0), 1)
    after = from_col(jnp.concatenate([left[:16], right[:16]], axis=0), -1)
    *weights, taps = weights_call(first_weight, second_weight, agg_weight, order)
    full, up, down, far = small_call(pack_kernel, k[None], (left, right, before, after), (WHOLE, EXACT, EXACT, TWO), (288, FULL), "pack_rows")
    across = to_band(full, 0, 1)
    above, below, twice = to_band(up, 1, 0), to_band(down, 3, 0), to_band(far, 2, 0)
    up, down = small_call(relay_kernel, k[None], (across,), (EXACT, EXACT), (FULL,), "relay_rows")
    rows = [full, across, above, below, twice, to_band(up, 1, 0), to_band(down, 3, 0), to_band(twice, 0, 1)]
    return main_call(jnp.stack([k, base]), rows, weights, taps)


def solution(mesh):
    return jax.shard_map(
        shards,
        mesh=mesh,
        in_specs=(P(None, "band", "col"), P(None, "band", "col"), P(), P(), P()),
        out_specs=P(None, "band", None, "col"),
        check_vma=False,
    )
```

```python
import functools

import jax
import jax.numpy as jnp
import numpy as np
from jax import lax
from jax.experimental import pallas as pl
from jax.experimental.pallas import tpu as pltpu
from jax.sharding import PartitionSpec as P

G, J, D, F, H, WL, BD, C, W = 40, 8, 192, 32, 8, 256, 24, 320, 4096
CH = J * H * G
REM = 144
ML, MR = 272, 288
LR, RR = 272, 296
NT = BD + 2
KT = 1024
UN = 8


def dot(x, w):
    return jnp.dot(x, w, preferred_element_type=jnp.float32)


def dot_on(x, i, y, j):
    return lax.dot_general(x, y, (((i,), (j,)), ((), ())), preferred_element_type=jnp.float32)


def build(dst, slot, src, m):
    for n in range(2):
        for e in range(3):
            dst[slot, :, (n * 3 + e) * 128:(n * 3 + e + 1) * 128] = src(n, e).astype(jnp.bfloat16)
    lane = lax.broadcasted_iota(jnp.int32, (m, 128), 1)
    pair = jnp.where(lane < 64, src(2, 0), pltpu.roll(src(2, 1), 64, 1))
    dst[slot, :, 768:896] = pair.astype(jnp.bfloat16)
    dst[slot, :, 896:960] = src(2, 2)[:, :64].astype(jnp.bfloat16)


def feature_view(m, at, k, base, xin, wm1, wr1, wm2, wr2, target, raw, xs, hs, ts, z, feat, wide):
    y = k & 1
    if at:
        start = window_start(k)
        formats = [(FULL, start)] * 2 + [(288, 0)] * 2 + [(PAIR, 24 - 24 * y), (288, 0), (288, 0), (PAIR, 24 - 24 * y)]
    else:
        formats = [(m, 0)] * 8
    source = [k, k ^ 1, (k + 6) & 7, (k + 2) & 7, (k + 4) & 7, ((k + 6) & 7) ^ 1, ((k + 2) & 7) ^ 1, ((k + 4) & 7) ^ 1]
    for d in range(8):
        h, (size, start) = source[d], formats[d]
        rem = REM if size == m else size // 2
        if size == m:
            uncut(raw.at[h], xin[d], at, m, rem)
        else:
            uncut(wide, xin[d], at, size, rem)
            for n in range(3):
                raw[h, n, 0:m, :] = wide[n, pl.ds(start, m), :]
    xs, hs, z, feat = xs.at[:, 0:m], hs.at[:, 0:m], z.at[:, :, 0:m], feat.at[:, :, 0:m]
    col = base + lax.broadcasted_iota(jnp.int32, (m, 128), 0)

    def rest(x, wr, h):
        y = dot(x[h + 1], wr[...])
        z[h + 1, 0] = y[:, :128]
        z[h + 1, 1, :, 0:64] = y[:, 128:192]

    def conv(x, wm, h):
        y = dot(x[h + 1], wm[1])
        if h > 0:
            y += dot(x[h], wm[0])
        if h < H - 1:
            y += dot(x[h + 2], wm[2])
        return y[:, :128], y[:, 128:], z[h, 0] + pltpu.roll(z[h + 1, 0], 64, 1) + z[h + 2, 1]

    def load(h, c):
        build(xs, h + 1, lambda n, e: raw[h, n, e:e + m, :], m)
        rest(xs, wr1, h)
        return c
    for h in range(H):
        load(h, 0)
    def first(i, c):
        for u in range(UN):
            first_row(UN * i + u, ts.at[u])
        return c
    def first_row(h, ts):
        ok = jnp.logical_and(col + 1 >= 0, col + 1 < W)
        for n, y in enumerate(conv(xs, wm1, h)):
            ts[n, 0:m, :] = jnp.where(ok, jnp.maximum(y, 0.0), 0.0)
        build(hs, h + 1, lambda n, e: ts[n, e:e + m, :], m)
    first(0, 0)
    def rest2(h, c):
        rest(hs, wr2, h)
        return c
    for h in range(H):
        rest2(h, 0)
    def second(h, c):
        ok = jnp.logical_and(col + 2 >= 0, col + 2 < W)
        for n, y in enumerate(conv(hs, wm2, h)):
            y = jnp.where(ok, y + raw[h, n, 2:2 + m, :], 0.0)
            feat[h, n] = y.astype(jnp.bfloat16).astype(jnp.float32)
        return c
    for h in range(H):
        second(h, 0)

    lane = lax.broadcasted_iota(jnp.int32, (16, 128), 1)
    def place(i, c):
        row = pl.multiple_of(i * 16, 16)
        for q in range(20):
            got = None
            for j in range(J):
                for h in range(H):
                    t0 = j * H * G + h * G
                    lo, hi = max(t0, q * 128), min(t0 + G, q * 128 + 128)
                    if lo >= hi:
                        continue
                    s_lo = lo - t0 + j * G
                    while lo < hi:
                        n = s_lo // 128
                        length = min(hi - lo, (n + 1) * 128 - s_lo)
                        x = feat[h, n, pl.ds(row, 16), :]
                        sh = (lo - s_lo) % 128
                        if sh:
                            x = pltpu.roll(x, sh, 1)
                        got = x if got is None else jnp.where(lane >= lo - q * 128, x, got)
                        lo, s_lo = lo + length, s_lo + length
            target[q, pl.ds(row, 16), :] = got
        return c
    lax.fori_loop(0, m // 16, place, 0, unroll=2)


def corr2(l_ref, r_ref, v_ref, p):
    def tile(i, c):
        row = pl.multiple_of(i * 8, 8)
        q = [[None] * 5 for _ in range(2)]
        for m in range(4):
            for n in range(5):
                lt = l_ref[m * 5 + n, pl.ds(row, 8), :]
                for u in range(2):
                    pr = lt * r_ref[m * 5 + n, pl.ds(row + (25 - u) - 2 * p, 8), :]
                    q[u][n] = pr if m == 0 else q[u][n] + pr
        for u in range(2):
            x = jnp.concatenate(q[u], axis=1)
            x = x + pltpu.roll(x, 320, 1)
            for n in range(3):
                v_ref[u, n, pl.ds(row, 8), :] = x[:, n * 128:n * 128 + 128]
        return c
    lax.fori_loop(0, 33, tile, 0, unroll=33)


def aggregate_views(k, b_ref, out_ref, lf_ref, rf_ref, v_ref, vs0, vs1, vs2):
    wide = lax.broadcasted_iota(jnp.int32, (WL, 128), 1)
    def pair(p, dst):
        corr2(lf_ref, rf_ref, v_ref, p)
        for u in range(2):
            def put(i, x, u=u):
                dst[:, u * KT + i * 128:u * KT + i * 128 + 128] = x.astype(jnp.bfloat16)
            for n in range(2):
                for e in range(3):
                    put(n * 3 + e, v_ref[u, n, e:e + WL, :])
            put(6, jnp.where(wide < 64, v_ref[u, 2, 0:WL, :], pltpu.roll(v_ref[u, 2, 1:1 + WL, :], 64, 1)))
            put(7, v_ref[u, 2, 2:2 + WL, :])
    def out(q, lo, hi):
        for u in range(2):
            if u == 0:
                y = jnp.dot(lo[...], b_ref[0:2 * KT], preferred_element_type=jnp.float32)
                y += jnp.dot(hi[:, 0:KT], b_ref[2 * KT:], preferred_element_type=jnp.float32)
            else:
                y = jnp.dot(lo[:, KT:], b_ref[0:KT], preferred_element_type=jnp.float32)
                y += jnp.dot(hi[...], b_ref[KT:], preferred_element_type=jnp.float32)
            y = jnp.maximum(y, 0.0).T.reshape(F, H, WL)
            out_ref[:, jnp.maximum(2 * q + u, 0)] = y.astype(jnp.bfloat16)
    bufs = (vs0, vs1, vs2)
    pair(0, vs0)
    @pl.when(k == 0)
    def _():
        vs0[:, 0:KT] = jnp.zeros((WL, KT), jnp.bfloat16)
    def three(i, c):
        for r in range(3):
            p = 1 + 3 * i + r
            new, lo, hi = bufs[(1 + r) % 3], bufs[(2 + r) % 3], bufs[r]
            out(p - 2, lo, hi)
            pair(p, new)
        return c
    lax.fori_loop(0, 4, three, 0)
    @pl.when(k == 7)
    def _():
        vs0[:, KT:] = jnp.zeros((WL, KT), jnp.bfloat16)
    out(11, vs2, vs0)


def order_matrix():
    to = np.arange(C)
    return jnp.asarray(np.arange(C)[:, None] == ((to % G) * J + to // G)[None, :], jnp.bfloat16)


def weights_kernel(w1, w2, aw, order, wm1, wr1, wm2, wr2, bt, tmp):
    lane = lax.broadcasted_iota(jnp.int32, (C, 128), 1)
    zero = jnp.zeros((C, 64), jnp.float32)
    for e in range(3):
        places = ((0, 128, e * 128), (128, 128, (3 + e) * 128), (256, 64, 768 + e * 64))
        for w, wm, wr, first in ((w1, wm1, wr1, True), (w2, wm2, wr2, False)):
            last = []
            for b in range(3):
                x = w[b * 3 + e]
                x = dot_on(order[...], 0, x, 1) if first else dot_on(x, 0, order[...], 0)
                for at, n, to in places:
                    wm[b, to:to + n, :] = x[at:at + n, :256].astype(jnp.bfloat16)
                last.append(jnp.concatenate([x[:, 256:320], zero], axis=1))
            pair = jnp.where(lane < 64, last[0], pltpu.roll(last[1], 64, 1)).astype(jnp.bfloat16)
            for at, n, to in places:
                wr[to:to + n, 0:128] = pair[at:at + n]
                wr[to:to + n, 128:192] = last[2][at:at + n, :64].astype(jnp.bfloat16)
    wide = lax.broadcasted_iota(jnp.int32, (F, 384), 1)
    for a in range(3):
        for e in range(3):
            x = [aw[(a * 3 + b) * 3 + e].astype(jnp.float32) for b in range(3)]
            x = jnp.concatenate(x + [jnp.zeros((F, 264), jnp.float32)], axis=1) * 0.125
            for ho in range(H):
                y = x if ho == 1 else pltpu.roll(x, ((ho - 1) * G) % 384, 1)
                y = jnp.where(wide < H * G, y, 0.0)
                for n in range(3):
                    tmp[n, pl.ds(ho, F, stride=H), :] = y[:, n * 128:n * 128 + 128]
            for n in range(2):
                at = a * KT + (n * 3 + e) * 128
                bt[at:at + 128, :] = tmp[n].T.astype(jnp.bfloat16)
            at, n = a * KT + 768 + e * 64, 64 if e < 2 else 128
            bt[at:at + n, :] = tmp[2].T[:n].astype(jnp.bfloat16)


def weights_call(w1, w2, aw, order):
    aw = aw.transpose(0, 1, 3, 2, 4).reshape(27, F, G)
    bf = lambda *s: jax.ShapeDtypeStruct(s, jnp.bfloat16)
    return pl.pallas_call(
        weights_kernel,
        out_shape=[bf(3, 960, 256), bf(960, 192), bf(3, 960, 256), bf(960, 192), bf(3 * KT, F * H)],
        scratch_shapes=[pltpu.VMEM((3, F * H, 128), jnp.float32)],
        compiler_params=pltpu.CompilerParams(vmem_limit_bytes=56 * 2**20),
        cost_estimate=pl.CostEstimate(flops=10_000_000, bytes_accessed=10_000_000, transcendentals=0),
        name="pack_weights",
    )(w1.reshape(9, C, C), w2.reshape(9, C, C), aw, order)

FULL, PAIR = 480, 320
LP = 2 * 272 + REM


def cut(dst, at, src, start, m, rem):
    for n in range(2):
        dst[at + n * m:at + n * m + m, :] = src[n, pl.ds(start, m), :].astype(jnp.bfloat16)
    lane = lax.broadcasted_iota(jnp.int32, (rem, 128), 1)
    pair = jnp.where(lane < 64, src[2, pl.ds(start, rem), :], pltpu.roll(src[2, pl.ds(start + m - rem, rem), :], 64, 1))
    dst[at + 2 * m:at + 2 * m + rem, :] = pair.astype(jnp.bfloat16)


def uncut(dst, src, at, m, rem):
    for n in range(2):
        dst[n, 0:m, :] = src[at + n * m:at + n * m + m, :].astype(jnp.float32)
    x = src[at + 2 * m:at + 2 * m + rem, :].astype(jnp.float32)
    dst[2, 0:rem, :] = x
    dst[2, m - rem:m, :] = pltpu.roll(x, 64, 1)


def window_start(k):
    return 181 - BD * k


def pack_kernel(k_ref, lt, rt, before, after, full, up, down, far, lext, rext):
    k = k_ref[0]
    f32 = lambda x: x.astype(jnp.float32)
    for n in range(3):
        w = 128 if n < 2 else 64
        col = slice(n * 128, n * 128 + w)
        lext[n, 0:16, :w] = f32(before[0:16, col])
        lext[n, 16:272, :w] = f32(lt[:, col])
        lext[n, 272:288, :w] = f32(after[0:16, col])
        rext[n, 0:208, :w] = f32(before[16:224, col])
        rext[n, 208:464, :w] = f32(rt[:, col])
        rext[n, 464:480, :w] = f32(after[16:32, col])
    for dst in (full, up, down, far):
        cut(dst, 0, lext, 13, 272, REM)
    cut(full, LP, rext, 0, FULL, FULL // 2)
    cut(up, LP, rext, window_start((k + 2) & 7), 288, REM)
    cut(down, LP, rext, window_start((k + 6) & 7), 288, REM)
    cut(far, LP, rext, window_start(((k + 4) & 7) | 1), PAIR, PAIR // 2)


def relay_kernel(k_ref, got, up, down, rext):
    k = k_ref[0]
    uncut(rext, got, LP, FULL, FULL // 2)
    for dst, to in ((up, (k + 2) & 7), (down, (k + 6) & 7)):
        dst[0:LP, :] = got[0:LP, :]
        cut(dst, LP, rext, window_start(to), 288, REM)


def rows_of(n):
    return jax.ShapeDtypeStruct((n, 128), jnp.bfloat16)

EXACT, WHOLE, TWO = LP + 720, LP + 1200, LP + 800


def small_call(kernel, k, args, outs, scratch, name):
    return pl.pallas_call(
        kernel,
        out_shape=[rows_of(n) for n in outs],
        in_specs=[pl.BlockSpec(memory_space=pltpu.SMEM)] + [pl.BlockSpec(memory_space=pltpu.VMEM)] * len(args),
        scratch_shapes=[pltpu.VMEM((3, n, 128), jnp.float32) for n in scratch],
        compiler_params=pltpu.CompilerParams(vmem_limit_bytes=32 * 2**20),
        cost_estimate=pl.CostEstimate(flops=2_000_000, bytes_accessed=3_000_000, transcendentals=0),
        name=name,
    )(k, *args)


def main_kernel(s_ref, *refs):
    xin, (wm1, wr1, wm2, wr2, taps, out_ref), scratch = refs[:8], refs[8:14], refs[14:]
    conv_scratch, (lf, rf, *others) = scratch[:7], scratch[7:]
    k, base = s_ref[0], s_ref[1]
    raw, xs, hs, ts, z = conv_scratch[:5]
    for slot in (0, 9):
        xs[slot] = jnp.zeros((MR, 960), jnp.bfloat16)
        hs[slot] = jnp.zeros((MR, 960), jnp.bfloat16)
        z[slot] = jnp.zeros((2, MR, 128), jnp.float32)
    feature_view(ML, 0, k, base - 3, xin, wm1, wr1, wm2, wr2, lf, *conv_scratch)
    feature_view(MR, LP, k, base - BD * k - 27, xin, wm1, wr1, wm2, wr2, rf, *conv_scratch)
    aggregate_views(k, taps, out_ref, lf, rf, *others)


def main_call(scal, rows, weights, taps):
    f32 = lambda *s: pltpu.VMEM(s, jnp.float32)
    b16 = lambda *s: pltpu.VMEM(s, jnp.bfloat16)
    return pl.pallas_call(
        main_kernel,
        out_shape=jax.ShapeDtypeStruct((F, BD, H, WL), jnp.bfloat16),
        in_specs=[pl.BlockSpec(memory_space=pltpu.SMEM)] + [pl.BlockSpec(memory_space=pltpu.VMEM)] * 13,
        out_specs=pl.BlockSpec(memory_space=pltpu.VMEM),
        scratch_shapes=[f32(8, 3, MR + 8, 128), b16(10, MR, 960), b16(10, MR, 960), f32(UN, 3, MR + 8, 128), f32(10, 2, MR, 128),
                        f32(8, 3, MR, 128), f32(3, FULL, 128), f32(20, LR, 128), f32(20, RR, 128), f32(2, 3, LR, 128),
                        b16(WL, 2 * KT), b16(WL, 2 * KT), b16(WL, 2 * KT)],
        compiler_params=pltpu.CompilerParams(vmem_limit_bytes=60 * 2**20),
        name="features_volume_aggregate",
    )(scal, *rows, *weights, taps)


def from_col(x, by):
    n = lax.axis_size("col")
    return lax.ppermute(x, "col", [(i, i + by) for i in range(n) if 0 <= i + by < n])


def to_band(x, z, y):
    n = lax.axis_size("band")
    return lax.ppermute(x, "band", [(i, ((i + 2 * z) % n) ^ y) for i in range(n)])


def shards(left_view, right_view, first_weight, second_weight, agg_weight):
    k = lax.axis_index("band").astype(jnp.int32)
    base = lax.axis_index("col").astype(jnp.int32) * WL
    order = order_matrix()
    left = dot_on(left_view[:, 0], 0, order, 0).astype(jnp.bfloat16)
    right = dot_on(right_view[:, 0], 0, order, 0).astype(jnp.bfloat16)
    before = from_col(jnp.concatenate([left[WL - 16:], right[WL - 208:]], axis=0), 1)
    after = from_col(jnp.concatenate([left[:16], right[:16]], axis=0), -1)
    *weights, taps = weights_call(first_weight, second_weight, agg_weight, order)
    full, up, down, far = small_call(pack_kernel, k[None], (left, right, before, after), (WHOLE, EXACT, EXACT, TWO), (288, FULL), "pack_rows")
    across = to_band(full, 0, 1)
    above, below, twice = to_band(up, 1, 0), to_band(down, 3, 0), to_band(far, 2, 0)
    up, down = small_call(relay_kernel, k[None], (across,), (EXACT, EXACT), (FULL,), "relay_rows")
    rows = [full, across, above, below, twice, to_band(up, 1, 0), to_band(down, 3, 0), to_band(far, 2, 1)]
    return main_call(jnp.stack([k, base]), rows, weights, taps)


def solution(mesh):
    return jax.shard_map(
        shards,
        mesh=mesh,
        in_specs=(P(None, "band", "col"), P(None, "band", "col"), P(), P(), P()),
        out_specs=P(None, "band", None, "col"),
        check_vma=False,
    )
```
